32 devices in a mesh: gx: 2 (over y), gy: 4 (over x, core), gz: 4 (over z).
Axes of the slice: x: 2, y: 2, z: 4, core: 2. Of those that a mesh axis runs over, the one named last changes fastest.
Arguments:
- density: float32 [8, 256, 512], P('gx', 'gy', 'gz'), may hold values from 0.18 to 1
- fixed_mask: int32 [8, 256, 512], P('gx', 'gy', 'gz'), may hold values 0 or 1
- load_mask: int32 [8, 256, 512], P('gx', 'gy', 'gz'), may hold values 0 or 1
- load_values: float32 [3, 8, 256, 512], P(None, 'gx', 'gy', 'gz'), may hold values from -7.5 to 7.5
Outputs:
- filtered: float32 [8, 256, 512], P('gx', 'gy', 'gz')
- displacement: float32 [3, 8, 256, 512], P(None, 'gx', 'gy', 'gz')
- residual: float32 [3, 8, 256, 512], P(None, 'gx', 'gy', 'gz')
The draws below stay inside these ranges and needn't reach their ends.
All inputs are finite; a program needn't handle non-finite values. No bound on the sum of `fixed_mask` or of `load_mask` on one device may be relied on, other than what follows from the above.
Results may differ from the reference program's by a relative error of at most 0.00035.
Values sent between devices are 32-bit elements; how exact they have to be, the bound alone decides.
No kernel may reach another device: no remote copies, remote signals or barrier semaphores. Data moves between devices by JAX's collectives and lax.ppermute only.
A program may use at most 128 MiB of HBM per device.

```python
import jax
import jax.numpy as jnp
import numpy as np

EX = 4
EY = 64
EZ = 128
FILTER_ITERS = 2
SOLVE_ITERS = 4
NX = 8
NY = 256
NZ = 512


def draw_density(key, part):
    key = jax.random.fold_in(key, 11)
    key_brick, key_noise = jax.random.split(key, 2)
    bricks = jax.random.uniform(key_brick, (NX // EX, NY // EY, NZ // EZ), jnp.float32, 0.5, 0.75)
    offsets = jnp.repeat(jnp.repeat(jnp.repeat(bricks, EX, axis=0), EY, axis=1), EZ, axis=2)
    pos_x = ((jnp.arange(NX, dtype=jnp.float32) + 0.5) / NX)[:, None, None]
    pos_y = ((jnp.arange(NY, dtype=jnp.float32) + 0.5) / NY)[None, :, None]
    pos_z = ((jnp.arange(NZ, dtype=jnp.float32) + 0.5) / NZ)[None, None, :]
    level = offsets * (0.6 + 0.4 * pos_x)
    amplitude = 0.25 * (0.3 + 0.7 * pos_x) * (0.5 + 0.5 * pos_y) * pos_z * pos_z
    noise = jax.random.uniform(key_noise, (NX, NY, NZ), jnp.float32, -1.0, 1.0)
    return level + amplitude * noise


def draw_load_values(key, part):
    ramp = (1.0 + 2.0 * jnp.arange(NX, dtype=jnp.float32) / (NX - 1))[None, :, None, None]
    base = jax.random.truncated_normal(key, -5.0, 5.0, (3, NX, NY, NZ), jnp.float32) * 0.5
    return ramp * base


def place_ends(entries, key, low, top_value):
    dims = entries.shape
    index_at = [jax.random.randint(jax.random.fold_in(key, axis), (), 0, dims[axis]) for axis in range(len(dims))]
    entries = entries.at[tuple(index_at)].set(low)
    longest = dims.index(max(dims))
    index_at[longest] = (index_at[longest] + 1) % dims[longest]
    return entries.at[tuple(index_at)].set(top_value)


def setup_inputs(seed: int = 0) -> dict:
    keys = jax.random.split(jax.random.key(seed), 5)
    return {
        "density": draw_density(jax.random.fold_in(keys[4], 71), 0),
        "fixed_mask": place_ends((jax.random.randint(keys[1], (NX, NY, NZ), 0, 16) < 1).astype(jnp.int32), jax.random.fold_in(keys[1], 1), 0, 1),
        "load_mask": place_ends((jax.random.randint(keys[2], (NX, NY, NZ), 0, 4) < 1).astype(jnp.int32), jax.random.fold_in(keys[2], 1), 0, 1),
        "load_values": draw_load_values(jax.random.fold_in(keys[4], 71), 0),
    }


MIN_MODULUS = 0.001
filter_weight = 0.75

def element_table():
    poisson = 0.3
    lame_first = poisson / ((1.0 + poisson) * (1.0 - 2.0 * poisson))
    lame_shear = 1.0 / (2.0 * (1.0 + poisson))
    elastic = np.zeros((6, 6))
    elastic[:3, :3] = lame_first
    for index in range(3):
        elastic[index, index] += 2.0 * lame_shear
        elastic[index + 3, index + 3] = lame_shear
    gauss_value = 1.0 / np.sqrt(3.0)
    matrix = np.zeros((24, 24))
    for first in (-gauss_value, gauss_value):
        for second in (-gauss_value, gauss_value):
            for third in (-gauss_value, gauss_value):
                gauss_point = (first, second, third)
                strain = np.zeros((6, 24))
                for corner in range(8):
                    corner_signs = [2 * (corner >> 2 & 1) - 1, 2 * (corner >> 1 & 1) - 1, 2 * (corner & 1) - 1]
                    factors = [1.0 + corner_signs[d] * gauss_point[d] for d in range(3)]
                    slopes = [corner_signs[d] * factors[(d + 1) % 3] * factors[(d + 2) % 3] / 4.0 for d in range(3)]
                    column = 3 * corner
                    strain[0, column] = slopes[0]
                    strain[1, column + 1] = slopes[1]
                    strain[2, column + 2] = slopes[2]
                    strain[3, column] = slopes[1]
                    strain[3, column + 1] = slopes[0]
                    strain[4, column + 1] = slopes[2]
                    strain[4, column + 2] = slopes[1]
                    strain[5, column] = slopes[2]
                    strain[5, column + 2] = slopes[0]
                matrix += strain.T @ elastic @ strain / 8.0
    return matrix.reshape(8, 3, 8, 3).transpose(0, 2, 1, 3)

def corner_offsets(corner):
    return (corner >> 2 & 1, corner >> 1 & 1, corner & 1)

def apply_stiffness(disp_pad, mod_pad, extent):
    stiffness = jnp.asarray(element_table(), jnp.float32)
    size_x, size_y, size_z = extent
    result = jnp.zeros((3, size_x, size_y, size_z), jnp.float32)
    for corner_a in range(8):
        offs_a = corner_offsets(corner_a)
        moduli_part = mod_pad[1 - offs_a[0]:1 - offs_a[0] + size_x, 1 - offs_a[1]:1 - offs_a[1] + size_y, 1 - offs_a[2]:1 - offs_a[2] + size_z]
        inner_sum = jnp.zeros((3, size_x, size_y, size_z), jnp.float32)
        for corner_b in range(8):
            offs_b = corner_offsets(corner_b)
            start_x = 1 - offs_a[0] + offs_b[0]
            start_y = 1 - offs_a[1] + offs_b[1]
            start_z = 1 - offs_a[2] + offs_b[2]
            shifted = disp_pad[:, start_x:start_x + size_x, start_y:start_y + size_y, start_z:start_z + size_z]
            for comp in range(3):
                inner_sum = inner_sum + stiffness[corner_a, corner_b, :, comp][:, None, None, None] * shifted[comp][None]
        result = result + moduli_part[None] * inner_sum
    return result

def jacobi_diagonal(mod_pad, extent):
    stiffness = jnp.asarray(element_table(), jnp.float32)
    size_x, size_y, size_z = extent
    diagonal = jnp.zeros((3, size_x, size_y, size_z), jnp.float32)
    for corner_a in range(8):
        offs_a = corner_offsets(corner_a)
        moduli_part = mod_pad[1 - offs_a[0]:1 - offs_a[0] + size_x, 1 - offs_a[1]:1 - offs_a[1] + size_y, 1 - offs_a[2]:1 - offs_a[2] + size_z]
        block_diag = jnp.stack([stiffness[corner_a, corner_a, comp, comp] for comp in range(3)])
        diagonal = diagonal + moduli_part[None] * block_diag[:, None, None, None]
    return diagonal

def face_sum(padded):
    beside = padded[2:, 1:-1, 1:-1] + padded[:-2, 1:-1, 1:-1]
    beside = beside + padded[1:-1, 2:, 1:-1] + padded[1:-1, :-2, 1:-1]
    return beside + padded[1:-1, 1:-1, 2:] + padded[1:-1, 1:-1, :-2]

def conjugate(operator, precond, force, iters):
    iterate = jnp.zeros_like(force)
    residual = force
    search = precond(residual)
    direction = search
    res_dot = jnp.sum(residual * search)
    for iteration in range(iters):
        image = operator(direction)
        step_size = res_dot / jnp.sum(direction * image)
        iterate = iterate + step_size * direction
        residual = residual - step_size * image
        if iteration + 1 < iters:
            search = precond(residual)
            new_dot = jnp.sum(residual * search)
            direction = search + new_dot / res_dot * direction
            res_dot = new_dot
    return (iterate, residual)

def reference(density, fixed_mask, load_mask, load_values):
    extent = density.shape
    counts = face_sum(jnp.pad(jnp.ones(extent, jnp.float32), 1))

    def filter_apply(field):
        return field + filter_weight * (counts * field - face_sum(jnp.pad(field, 1)))

    def identity(field):
        return field
    filtered, unused = conjugate(filter_apply, identity, density, FILTER_ITERS)
    moduli = MIN_MODULUS + (1.0 - MIN_MODULUS) * filtered * filtered * jnp.abs(filtered)
    mod_pad = jnp.pad(moduli, 1)
    free_nodes = (1 - fixed_mask).astype(jnp.float32)
    force = free_nodes[None] * load_mask.astype(jnp.float32)[None] * load_values
    inverse_diag = free_nodes[None] / jacobi_diagonal(mod_pad, extent)

    def elastic_apply(field):
        disp_pad = jnp.pad(field, ((0, 0), (1, 1), (1, 1), (1, 1)))
        return free_nodes[None] * apply_stiffness(disp_pad, mod_pad, extent)

    def jacobi(field):
        return inverse_diag * field
    displacement, residual = conjugate(elastic_apply, jacobi, force, SOLVE_ITERS)
    return (filtered, displacement, residual)
```

```python
import functools

import jax
import jax.numpy as jnp
import numpy as np
from jax import lax
from jax.experimental import pallas as pl
from jax.experimental.pallas import tpu as pltpu
from jax.sharding import PartitionSpec as P

FILTER_ITERS = 2
SOLVE_ITERS = 4


MIN_MODULUS = 0.001
filter_weight = 0.75


def passed_along(value, axis, steps):
    count = lax.axis_size(axis)
    initial, last = (max(0, -steps), min(count, count - steps))
    return lax.ppermute(value, axis, [(source, source + steps) for source in range(initial, last)])


def padded_2(block, sides, width):
    for axis, dim in sides:
        count = lax.axis_size(axis)
        forward = [(i, i + 1) for i in range(count - 1)]
        backward = [(target, source) for source, target in forward]
        low = lax.ppermute(
            lax.slice_in_dim(block, block.shape[dim] - width, None, axis=dim), axis, forward
        )
        high = lax.ppermute(lax.slice_in_dim(block, 0, width, axis=dim), axis, backward)
        block = jnp.concatenate([low, block, high], axis=dim)
    return block


def element_table():
    poisson = 0.3
    lame_first = poisson / ((1.0 + poisson) * (1.0 - 2.0 * poisson))
    lame_shear = 1.0 / (2.0 * (1.0 + poisson))
    elastic = np.zeros((6, 6))
    elastic[:3, :3] = lame_first
    for index in range(3):
        elastic[index, index] += 2.0 * lame_shear
        elastic[index + 3, index + 3] = lame_shear
    gauss_value = 1.0 / np.sqrt(3.0)
    matrix = np.zeros((24, 24))
    for first in (-gauss_value, gauss_value):
        for second in (-gauss_value, gauss_value):
            for third in (-gauss_value, gauss_value):
                gauss_point = (first, second, third)
                strain = np.zeros((6, 24))
                for corner in range(8):
                    corner_signs = [
                        2 * (corner >> 2 & 1) - 1,
                        2 * (corner >> 1 & 1) - 1,
                        2 * (corner & 1) - 1,
                    ]
                    factors = [1.0 + corner_signs[d] * gauss_point[d] for d in range(3)]
                    slopes = [
                        corner_signs[d] * factors[(d + 1) % 3] * factors[(d + 2) % 3] / 4.0
                        for d in range(3)
                    ]
                    column = 3 * corner
                    strain[0, column] = slopes[0]
                    strain[1, column + 1] = slopes[1]
                    strain[2, column + 2] = slopes[2]
                    strain[3, column] = slopes[1]
                    strain[3, column + 1] = slopes[0]
                    strain[4, column + 1] = slopes[2]
                    strain[4, column + 2] = slopes[1]
                    strain[5, column] = slopes[2]
                    strain[5, column + 2] = slopes[0]
                matrix += strain.T @ elastic @ strain / 8.0
    return matrix.reshape(8, 3, 8, 3).transpose(0, 2, 1, 3)


def corner_offsets(corner):
    return (corner >> 2 & 1, corner >> 1 & 1, corner & 1)


def apply_stiffness(disp_pad, mod_pad, extent):
    stiffness = jnp.asarray(element_table(), jnp.float32)
    size_x, size_y, size_z = extent
    result = jnp.zeros((3, size_x, size_y, size_z), jnp.float32)
    for corner_a in range(8):
        offs_a = corner_offsets(corner_a)
        moduli_part = mod_pad[
            1 - offs_a[0] : 1 - offs_a[0] + size_x,
            1 - offs_a[1] : 1 - offs_a[1] + size_y,
            1 - offs_a[2] : 1 - offs_a[2] + size_z,
        ]
        inner_sum = jnp.zeros((3, size_x, size_y, size_z), jnp.float32)
        for corner_b in range(8):
            offs_b = corner_offsets(corner_b)
            start_x = 1 - offs_a[0] + offs_b[0]
            start_y = 1 - offs_a[1] + offs_b[1]
            start_z = 1 - offs_a[2] + offs_b[2]
            shifted = disp_pad[
                :,
                start_x : start_x + size_x,
                start_y : start_y + size_y,
                start_z : start_z + size_z,
            ]
            for comp in range(3):
                inner_sum = (
                    inner_sum
                    + stiffness[corner_a, corner_b, :, comp][:, None, None, None]
                    * shifted[comp][None]
                )
        result = result + moduli_part[None] * inner_sum
    return result


def jacobi_diagonal(mod_pad, extent):
    stiffness = jnp.asarray(element_table(), jnp.float32)
    size_x, size_y, size_z = extent
    diagonal = jnp.zeros((3, size_x, size_y, size_z), jnp.float32)
    for corner_a in range(8):
        offs_a = corner_offsets(corner_a)
        moduli_part = mod_pad[
            1 - offs_a[0] : 1 - offs_a[0] + size_x,
            1 - offs_a[1] : 1 - offs_a[1] + size_y,
            1 - offs_a[2] : 1 - offs_a[2] + size_z,
        ]
        block_diag = jnp.stack([stiffness[corner_a, corner_a, comp, comp] for comp in range(3)])
        diagonal = diagonal + moduli_part[None] * block_diag[:, None, None, None]
    return diagonal


def face_sum(padded):
    beside = padded[2:, 1:-1, 1:-1] + padded[:-2, 1:-1, 1:-1]
    beside = beside + padded[1:-1, 2:, 1:-1] + padded[1:-1, :-2, 1:-1]
    return beside + padded[1:-1, 1:-1, 2:] + padded[1:-1, 1:-1, :-2]


def edge_count(global_index, total):
    return (global_index > 0).astype(jnp.float32) + (global_index < total - 1).astype(jnp.float32)


def neighbour_counts(extent):
    size_x, size_y, size_z = extent
    index_x = lax.axis_index("gx") * size_x + jnp.arange(size_x, dtype=jnp.int32)
    index_y = lax.axis_index("gy") * size_y + jnp.arange(size_y, dtype=jnp.int32)
    index_z = lax.axis_index("gz") * size_z + jnp.arange(size_z, dtype=jnp.int32)
    count_x = edge_count(index_x, size_x * lax.axis_size("gx"))
    count_y = edge_count(index_y, size_y * lax.axis_size("gy"))
    count_z = edge_count(index_z, size_z * lax.axis_size("gz"))
    return count_x[:, None, None] + count_y[None, :, None] + count_z[None, None, :]


def lower_moduli(moduli):
    rim_x = passed_along(moduli[-1:], "gx", 1)
    extended = jnp.concatenate([rim_x, moduli], axis=0)
    rim_y = passed_along(extended[:, -1:], "gy", 1)
    extended = jnp.concatenate([rim_y, extended], axis=1)
    rim_z = passed_along(extended[:, :, -1:], "gz", 1)
    return jnp.concatenate([rim_z, extended], axis=2)


def displacement_halo(field):
    return padded_2(field, (("gx", 1), ("gy", 2), ("gz", 3)), 1)


def residual_dot(first, second):
    return lax.psum(jnp.sum(first * second), ("gx", "gy", "gz"))


def curvature_dot(first, second):
    return lax.psum(jnp.sum(first * second), ("gx", "gy", "gz"))


def conjugate(operator, precond, force, iters):
    iterate = jnp.zeros_like(force)
    residual = force
    search = precond(residual)
    direction = search
    res_dot = residual_dot(residual, search)
    for iteration in range(iters):
        image = operator(direction)
        step_size = res_dot / curvature_dot(direction, image)
        iterate = iterate + step_size * direction
        residual = residual - step_size * image
        if iteration + 1 < iters:
            search = precond(residual)
            new_dot = residual_dot(residual, search)
            direction = search + new_dot / res_dot * direction
            res_dot = new_dot
    return (iterate, residual)


def general_shards(density, fixed_mask, load_mask, load_values):
    extent = density.shape
    counts = neighbour_counts(extent)

    def filter_apply(field):
        padded = padded_2(field, (("gx", 0), ("gy", 1), ("gz", 2)), 1)
        return field + filter_weight * (counts * field - face_sum(padded))

    def identity(field):
        return field

    filtered, unused = conjugate(filter_apply, identity, density, FILTER_ITERS)
    moduli = MIN_MODULUS + (1.0 - MIN_MODULUS) * filtered * filtered * jnp.abs(filtered)
    mod_pad = lower_moduli(moduli)
    free_nodes = (1 - fixed_mask).astype(jnp.float32)
    force = free_nodes[None] * load_mask.astype(jnp.float32)[None] * load_values
    inverse_diag = free_nodes[None] / jacobi_diagonal(mod_pad, extent)

    def elastic_apply(field):
        return free_nodes[None] * apply_stiffness(displacement_halo(field), mod_pad, extent)

    def jacobi(field):
        return inverse_diag * field

    displacement, residual = conjugate(elastic_apply, jacobi, force, SOLVE_ITERS)
    return (filtered, displacement, residual)


HALO = 4
SW = 16
FACE = 8
PARTS = 8
AXES = ("gx", "gy", "gz")
SHIFTS = (1.2, 0.4, 2.0, 0.8)
VMEM_LIMIT = 24 * 1024 * 1024
POISSON = 0.3
LAME = POISSON / ((1.0 + POISSON) * (1.0 - 2.0 * POISSON))
SHEAR = 1.0 / (2.0 * (1.0 + POISSON))
AXIAL = LAME + 2.0 * SHEAR
MODES = [(a, b, g) for a in range(2) for b in range(2) for g in range(2)]


def lanes_of(shape):
    return lax.broadcasted_iota(jnp.int32, shape, len(shape) - 1)


def rows_of(shape):
    return lax.broadcasted_iota(jnp.int32, shape, len(shape) - 2)


def turned(value, shift, axis):
    size = value.shape[axis]
    if isinstance(shift, int):
        shift = shift % size
        if shift == 0:
            return value
    else:
        shift = lax.rem(shift + 4 * size, size)
    return pltpu.roll(value, shift, axis)


def either(flag, first, second):
    return jnp.where(jnp.full(first.shape, flag, jnp.int32) == 0, first, second)


def pack_kernel(density, fixed, load_mask, load_values, fields, send_a, send_b):
    planes, rows, _ = density.shape
    odd = lax.rem(lax.axis_index("gy"), 2)
    for p in range(planes):
        free = (1 - fixed[p]).astype(jnp.float32)
        loaded = free * load_mask[p].astype(jnp.float32)
        fields[p] = density[p]
        fields[planes + p] = free
        for c in range(3):
            fields[(2 + c) * planes + p] = loaded * load_values[c, p]
    row_a = pl.multiple_of((1 - odd) * (rows - FACE), FACE)
    row_b = pl.multiple_of(odd * (rows - FACE), FACE)
    send_a[...] = fields[:, pl.ds(row_a, FACE), :]
    send_b[...] = fields[:, pl.ds(row_b, FACE), :]


def strip_kernel(fields, from_a, from_b, density_out, node_out, own, send_a, send_b):
    total, rows, lanes = fields.shape
    planes = total // 5
    odd_y = lax.rem(lax.axis_index("gy"), 2)
    odd_z = lax.rem(lax.axis_index("gz"), 2)
    row = rows_of((FACE, lanes))
    for q in range(total):
        above = either(odd_y, from_a[q], from_b[q])
        below = either(odd_y, from_b[q], from_a[q])
        if q < planes:
            density_out[q, :rows] = fields[q]
            density_out[q, rows : rows + FACE] = above
            density_out[q, rows + FACE :] = below
        else:
            node_out[q - planes, :rows] = fields[q]
            node_out[q - planes, rows:] = jnp.where(row < HALO, above, below)
    wide = rows + 2 * FACE
    tall = rows + FACE
    own[:wide] = jnp.zeros((wide, lanes), jnp.float32)
    lane = lanes_of((wide, lanes))
    low = jnp.zeros((wide, lanes), jnp.float32)
    high = low
    for p in range(planes):
        value = density_out[p]
        base = SW * p
        low = jnp.where((lane >= base) & (lane < base + 8), turned(value, base, 1), low)
        high = jnp.where((lane >= base + 8) & (lane < base + 16), turned(value, base + 16, 1), high)
    send_a[:wide] = either(odd_z, high, low)
    send_b[:wide] = either(odd_z, low, high)
    lane = lanes_of((tall, lanes))
    for pair in range(2):
        low = jnp.zeros((tall, lanes), jnp.float32)
        high = low
        mine = low
        for half in range(2):
            for p in range(planes):
                value = node_out[(2 * pair + half) * planes + p]
                base = SW * p + (lanes // 2) * half
                four = turned(value, base + 4, 1)
                twelve = turned(value, base + 12, 1)
                part = (lane - base) // 4
                inside = (lane >= base) & (lane < base + SW)
                mine = jnp.where(inside & (part == 0), four, mine)
                low = jnp.where(inside & (part == 1), four, low)
                high = jnp.where(inside & (part == 2), twelve, high)
                mine = jnp.where(inside & (part == 3), twelve, mine)
        at = wide + pair * tall
        own[at : at + tall] = mine
        send_a[at : at + tall] = either(odd_z, high, low)
        send_b[at : at + tall] = either(odd_z, low, high)


def filter_kernel(grid, own, other, strip_own, strip_other, window, first, strip_v, strip_g, dots):
    planes, wide, lanes = own.shape
    rows = wide - 2 * FACE
    count = 2 * planes
    total_y, total_z = grid
    gx = lax.axis_index("gx")
    base_y = lax.axis_index("gy") * rows
    base_z = lax.axis_index("gz") * lanes
    mine = gx * planes
    window[pl.ds(mine, planes)] = own[...]
    window[pl.ds(planes - mine, planes)] = other[...]
    shape = (wide, lanes)
    lane = lanes_of(shape)
    row = rows_of(shape)
    lower = either(gx, strip_own[:wide], strip_other[:wide])
    upper = either(gx, strip_other[:wide], strip_own[:wide])
    strip_v[...] = jnp.where(lane < lanes // 2, lower, turned(upper, lanes // 2, 1))
    at_y = base_y + jnp.where(row < rows + FACE, row, row - wide)
    pass_y = ((at_y >= 0) & (at_y < total_y - 1)).astype(jnp.float32)
    pass_z = (base_z + lane < total_z - 1).astype(jnp.float32)
    back_z = (base_z + lane > 0).astype(jnp.float32)
    place = lax.rem(lane, SW)
    at_strip = base_z + jnp.where(place < 8, lanes + place, place - SW)
    strip_pass = ((at_strip >= 0) & (at_strip < total_z - 1)).astype(jnp.float32)
    strip_back = ((at_strip >= 1) & (at_strip < total_z)).astype(jnp.float32)

    def along_y(value):
        ahead = (turned(value, -1, 0) - value) * pass_y
        return turned(ahead, 1, 0) - ahead

    def laplace(source, strip, p):
        value = source[p]
        result = (value - source[jnp.minimum(p + 1, count - 1)]) + (value - source[jnp.maximum(p - 1, 0)])
        result = result + along_y(value)
        side = strip[...]
        ahead = jnp.where(lane == lanes - 1, turned(side, lanes - 1 - SW * p, 1), turned(value, -1, 1))
        behind = jnp.where(lane == 0, turned(side, 0 - (SW * p + SW - 1), 1), turned(value, 1, 1))
        result = result + (value - ahead) * pass_z + (value - behind) * back_z
        return filter_weight * result

    def first_plane(p, carry):
        first[p] = laplace(window, strip_v, p)
        return carry

    lax.fori_loop(0, count, first_plane, 0)
    value = strip_v[...]
    edge_low = jnp.zeros(shape, jnp.float32)
    edge_high = edge_low
    for p in range(count):
        edge_low = jnp.where(lane == SW * p + SW - 1, turned(window[p], SW * p + SW - 1, 1), edge_low)
        edge_high = jnp.where(lane == SW * p, turned(window[p], SW * p - (lanes - 1), 1), edge_high)
    ahead = jnp.where(place == SW - 1, edge_low, turned(value, -1, 1))
    behind = jnp.where(place == 0, edge_high, turned(value, 1, 1))
    result = along_y(value) + (value - ahead) * strip_pass + (value - behind) * strip_back
    ahead = jnp.where(lane < lanes - SW, turned(value, -SW, 1) - value, 0.0)
    result = result + turned(ahead, SW, 1) - ahead
    strip_g[...] = filter_weight * result

    def add_dots(p, sums):
        plane = mine + p
        w = window[plane][:rows]
        g = first[plane][:rows]
        gg = laplace(first, strip_g, plane)[:rows]
        terms = (w * w, w * g, g * g, g * gg)
        return tuple(
            s + jnp.sum(t.reshape(rows // 8, 8, lanes), axis=0) for s, t in zip(sums, terms)
        )

    zero = jnp.zeros((8, lanes), jnp.float32)
    spread(lax.fori_loop(0, planes, add_dots, (zero,) * 4), dots)


def spread(sums, dots):
    lanes = dots.shape[-1]
    lane = lanes_of((1, lanes))
    line = jnp.zeros((1, lanes), jnp.float32)
    for k, value in enumerate(sums):
        value = jnp.sum(jnp.sum(value, axis=0, keepdims=True), axis=1, keepdims=True)
        line = jnp.where(lane == k, value, line)
    for k in range(dots.shape[0]):
        dots[k] = line


def gathered(dots, count):
    line = jnp.sum(dots[...], axis=0)
    lane = lanes_of(line.shape)
    return [
        jnp.sum(jnp.where(lane == k, line, 0.0), axis=1, keepdims=True) for k in range(count)
    ]


def element_forces(u, modulus):
    shear = modulus * (SHEAR / 16.0)
    shear_3 = modulus * (SHEAR / 48.0)
    twist = modulus * ((AXIAL + 2.0 * SHEAR) / 144.0)
    normal = modulus * (2.0 * SHEAR / 16.0)
    paired = modulus * ((AXIAL + SHEAR) / 48.0)
    x, y, z = u
    f = [{}, {}, {}]
    trace = (x[1, 0, 0] + y[0, 1, 0] + z[0, 0, 1]) * (LAME / (2.0 * SHEAR))
    f[0][1, 0, 0] = (trace + x[1, 0, 0]) * normal
    f[1][0, 1, 0] = (trace + y[0, 1, 0]) * normal
    f[2][0, 0, 1] = (trace + z[0, 0, 1]) * normal
    ratio = LAME / (AXIAL + SHEAR)
    for (c, m), (d, n) in (
        ((0, (1, 1, 0)), (2, (0, 1, 1))),
        ((1, (1, 1, 0)), (2, (1, 0, 1))),
        ((0, (1, 0, 1)), (1, (0, 1, 1))),
    ):
        f[c][m] = (u[c][m] + ratio * u[d][n]) * paired
        f[d][n] = (u[d][n] + ratio * u[c][m]) * paired
    for (c, m), (d, n) in (
        ((0, (0, 1, 0)), (1, (1, 0, 0))),
        ((1, (0, 0, 1)), (2, (0, 1, 0))),
        ((0, (0, 0, 1)), (2, (1, 0, 0))),
    ):
        f[c][m] = f[d][n] = (u[c][m] + u[d][n]) * shear
    three = ((0, (0, 1, 1)), (1, (1, 0, 1)), (2, (1, 1, 0)))
    both = x[0, 1, 1] + y[1, 0, 1] + z[1, 1, 0]
    for c, m in three:
        f[c][m] = (both + u[c][m]) * shear_3
    for c in range(3):
        f[c][1, 1, 1] = u[c][1, 1, 1] * twist
    return f


def solve_kernel(
    grid, diagonal, window, first, strip_v, strip_g, filter_dots, node_own, node_other, strip_own, strip_other,
    filtered, basis, scale, dots,
    modulus, inverse, free, fields, pairs, kept, carried, near, far,
    s_modulus, s_inverse, s_free, s_old, s_disp, s_near, s_far, s_edge,
):
    count, wide, lanes = window.shape
    rows = wide - 2 * FACE
    tall = rows + FACE
    tiles = tall // 8
    planes = count // 2
    total_y, total_z = grid
    gx = lax.axis_index("gx")
    base_y = lax.axis_index("gy") * rows
    base_z = lax.axis_index("gz") * lanes
    mine = gx * planes

    a, b, c, e = gathered(filter_dots, 4)
    step = a / (a + b)
    beta = step * step * (c - b * b / a) / a
    to_v = step * b / a + beta
    to_g = -step
    bottom = to_v * to_v * (a + b) + 2.0 * to_v * to_g * (b + c) + to_g * to_g * (c + e)
    second = beta * a / bottom
    weight_v = step + second * to_v
    weight_g = second * to_g

    shape = (wide, lanes)
    lane = lanes_of(shape)
    row = rows_of(shape)
    at_y = base_y + jnp.where(row < rows + FACE, row, row - wide)
    inside_y = (at_y >= 0) & (at_y < total_y)
    place = lax.rem(lane, SW)
    at_strip = base_z + jnp.where(place < 8, lanes + place, place - SW)
    inside_strip = inside_y & (at_strip >= 0) & (at_strip < total_z)
    small = rows_of((8, lanes))

    def folded(value):
        tail = jnp.where(small < HALO, value[rows : rows + 8], value[rows + 8 :])
        return value[:rows], tail

    def put(ref, index, value):
        head, tail = folded(value)
        ref[index, :rows] = head
        ref[index, rows:] = tail

    def moduli_of(v, g):
        value = weight_v * v + weight_g * g
        return value, MIN_MODULUS + (1.0 - MIN_MODULUS) * value * value * jnp.abs(value)

    side = moduli_of(strip_v[...], strip_g[...])[1]
    side = jnp.where(inside_strip, side, 0.0)

    def inverted(total, open_nodes):
        return jnp.where(total > 0.0, open_nodes / jnp.where(total > 0.0, diagonal * total, 1.0), 0.0)

    node_at = [pl.ds(pl.multiple_of(mine, planes), planes), pl.ds(pl.multiple_of(planes - mine, planes), planes)]
    for f in range(4):
        for source, at in zip((node_own, node_other), node_at):
            value = source[f * planes : (f + 1) * planes]
            if f == 0:
                free[at] = value
            else:
                basis[0, f - 1, at] = value

    s_line = jnp.zeros(shape, jnp.float32)
    previous = jnp.zeros(shape, jnp.float32)
    for p in range(count):
        value, mod = moduli_of(window[p], first[p])
        mod = jnp.where(inside_y, mod, 0.0)
        put(modulus, p, mod)
        edge = turned(side, 0 - (SW * p + SW - 1), 1)
        across = mod + jnp.where(lane == 0, edge, turned(mod, 1, 1))
        across = across + turned(across, 1, 0)
        head, tail = folded(across + previous)
        previous = across
        inverse[p, :rows] = inverted(head, free[p, :rows])
        inverse[p, rows:] = inverted(tail, free[p, rows:])
        s_line = jnp.where((lane >= SW * p) & (lane < SW * p + 4), turned(mod, SW * p + 4, 1), s_line)
        s_line = jnp.where((lane >= SW * p + 12) & (lane < SW * p + 16), turned(mod, SW * p + 12, 1), s_line)
    for p in range(planes):
        v = window[mine + p]
        g = first[mine + p]
        filtered[p] = (weight_v * v + weight_g * g)[:rows]

    s_mod = jnp.where(
        (place >= 4) & (place < 8), turned(side, 4, 1), jnp.where((place >= 8) & (place < 12), turned(side, -4, 1), s_line)
    )
    put(s_modulus, 0, s_mod)
    across = s_mod + jnp.where(place == 8, turned(side, -3, 1), turned(s_mod, 1, 1))
    across = across + turned(across, 1, 0)
    across = across + jnp.where(lane < SW, 0.0, turned(across, SW, 1))
    s_head, s_tail = folded(across)

    half = lanes // 2
    for pair in range(2):
        at = wide + pair * tall
        lower = either(gx, strip_own[at : at + tall], strip_other[at : at + tall])
        upper = either(gx, strip_other[at : at + tall], strip_own[at : at + tall])
        left = lanes_of((tall, lanes)) < half
        one = jnp.where(left, lower, turned(upper, half, 1))
        two = jnp.where(left, turned(lower, half, 1), upper)
        for k, value in ((2 * pair, one), (2 * pair + 1, two)):
            if k == 0:
                s_free[...] = value
            else:
                s_old[k - 1] = value
    s_inverse[:rows] = inverted(s_head, s_free[:rows])
    s_inverse[rows:] = inverted(s_tail, s_free[rows:])
    for c in range(3):
        s_disp[0, c, :tall] = s_inverse[...] * s_old[c]
        s_disp[0, c, tall : tall + 1] = s_disp[0, c, 0:1]

    lane = lanes_of((8, lanes))
    last_plane = lane >= lanes - SW
    first_plane = lane < SW

    for j in range(4):
        for t in range(tiles):
            r = 8 * t
            u = []
            for c in range(3):
                now = s_disp[j, c, r : r + 8]
                after = s_disp[j, c, r + 1 : r + 9]
                modes = {}
                for beta_, value in ((0, now + after), (1, after - now)):
                    beside = jnp.where(last_plane, 0.0, turned(value, -SW, 1))
                    for alpha, across in ((0, value + beside), (1, beside - value)):
                        next_z = turned(across, -1, 1)
                        if (alpha, beta_) != (0, 0):
                            modes[alpha, beta_, 0] = across + next_z
                        modes[alpha, beta_, 1] = next_z - across
                u.append(modes)
            f = element_forces(u, s_modulus[0, r : r + 8])
            for c in range(3):
                for g in range(2):
                    t_beta = []
                    for beta_ in range(2):
                        diff = f[c][1, beta_, g]
                        if (beta_, g) == (0, 0):
                            lower, upper = -diff, diff
                        else:
                            total = f[c][0, beta_, g]
                            lower, upper = total - diff, total + diff
                        t_beta.append(lower + jnp.where(first_plane, 0.0, turned(upper, SW, 1)))
                    s_near[2 * c + g, r : r + 8] = t_beta[0] - t_beta[1]
                    s_far[2 * c + g, r + 8 : r + 16] = t_beta[0] + t_beta[1]
        for k in range(6):
            s_far[k, 7:8] = s_far[k, tall + 7 : tall + 8]
        for t in range(tiles):
            r = 8 * t
            for c in range(3):
                total = s_near[2 * c, r : r + 8] + s_far[2 * c, r + 7 : r + 15]
                diff = s_near[2 * c + 1, r : r + 8] + s_far[2 * c + 1, r + 7 : r + 15]
                upper = total + diff
                s_edge[j, c, r : r + 8] = upper
                if j < 3:
                    out = (total - diff) + turned(upper, 1, 1)
                    new = s_free[r : r + 8] * out - SHIFTS[j] * s_old[c, r : r + 8]
                    s_old[c, r : r + 8] = new
                    s_disp[j + 1, c, r : r + 8] = s_inverse[r : r + 8] * new
        if j < 3:
            for c in range(3):
                s_disp[j + 1, c, tall : tall + 1] = s_disp[j + 1, c, 0:1]

    def spread_z(j, c, p, r, disp):
        edge = turned(s_disp[j, c, r : r + 8], lanes - 1 - (SW * p + 4), 1)
        ahead = jnp.where(lane == lanes - 1, edge, turned(disp, -1, 1))
        pairs[2 * c, p, r : r + 8] = disp + ahead
        pairs[2 * c + 1, p, r : r + 8] = ahead - disp

    def close_rows(p):
        for k in range(6):
            pairs[k, p, tall : tall + 1] = pairs[k, p, 0:1]

    for k in range(6):
        pairs[k, count] = jnp.zeros(pairs.shape[2:], jnp.float32)

    def start_plane(p, carry):
        for t in range(tiles):
            r = 8 * t
            for c in range(3):
                spread_z(0, c, p, r, inverse[p, r : r + 8] * basis[0, c, p, r : r + 8])
        close_rows(p)
        return carry

    lax.fori_loop(0, count, start_plane, 0)

    def along_rows(p, r):
        result = []
        for k in range(6):
            now = pairs[k, p, r : r + 8]
            after = pairs[k, p, r + 1 : r + 9]
            result.append((now + after, after - now))
        return result

    for j in range(4):
        low = gx * j
        high = count - 1 - j + gx * (j + 1)
        for t in range(tiles):
            r = 8 * t
            for k, both in enumerate(along_rows(low, r)):
                for beta_ in range(2):
                    kept[2 * k + beta_, r : r + 8] = both[beta_]
                    carried[2 * k + beta_, r : r + 8] = jnp.zeros((8, lanes), jnp.float32)

        def layer(p, state, j=j):
            for t in range(tiles):
                r = 8 * t
                upper_rows = along_rows(p + 1, r)
                u = []
                for c in range(3):
                    modes = {}
                    for g in range(2):
                        for beta_ in range(2):
                            k = 2 * (2 * c + g) + beta_
                            now = kept[k, r : r + 8]
                            above = upper_rows[2 * c + g][beta_]
                            if (beta_, g) != (0, 0):
                                modes[0, beta_, g] = now + above
                            modes[1, beta_, g] = above - now
                            kept[k, r : r + 8] = above
                    u.append(modes)
                f = element_forces(u, modulus[p, r : r + 8])
                for c in range(3):
                    for g in range(2):
                        t_beta = []
                        for beta_ in range(2):
                            k = 2 * (2 * c + g) + beta_
                            diff = f[c][1, beta_, g]
                            before = carried[k, r : r + 8]
                            if (beta_, g) == (0, 0):
                                t_beta.append(before - diff)
                                carried[k, r : r + 8] = diff
                            else:
                                total = f[c][0, beta_, g]
                                t_beta.append(before + (total - diff))
                                carried[k, r : r + 8] = total + diff
                        near[2 * c + g, r : r + 8] = t_beta[0] - t_beta[1]
                        far[2 * c + g, r + 8 : r + 16] = t_beta[0] + t_beta[1]
            for k in range(6):
                far[k, 7:8] = far[k, tall + 7 : tall + 8]
            for t in range(tiles):
                r = 8 * t
                open_nodes = free[p, r : r + 8]
                inv = inverse[p, r : r + 8]
                for c in range(3):
                    total = near[2 * c, r : r + 8] + far[2 * c, r + 7 : r + 15]
                    diff = near[2 * c + 1, r : r + 8] + far[2 * c + 1, r + 7 : r + 15]
                    edge = turned(s_edge[j, c, r : r + 8], 0 - (SW * p + 11), 1)
                    out = (total - diff) + jnp.where(lane == 0, edge, turned(total + diff, 1, 1))
                    new = open_nodes * out - SHIFTS[j] * basis[j, c, p, r : r + 8]
                    basis[j + 1, c, p, r : r + 8] = new
                    if j < 3:
                        spread_z(j + 1, c, p, r, inv * new)
            if j < 3:
                close_rows(p)
            return state

        lax.fori_loop(low, high, layer, 0)

    order = [(i, k) for i in range(4) for k in range(i, 5)]

    def add_dots(p, sums):
        plane = mine + p
        sums = list(sums)
        for t in range(rows // 8):
            r = 8 * t
            inv = inverse[plane, r : r + 8]
            scale[p, r : r + 8] = inv
            for c in range(3):
                ys = [basis[i, c, plane, r : r + 8] for i in range(5)]
                ws = [inv * y for y in ys[:4]]
                for i in range(5):
                    fields[i, c, p, r : r + 8] = ys[i]
                for n, (i, k) in enumerate(order):
                    sums[n] = sums[n] + ws[i] * ys[k]
        return tuple(sums)

    zero = jnp.zeros((8, lanes), jnp.float32)
    spread(lax.fori_loop(0, planes, add_dots, (zero,) * len(order)), dots)


def combine_kernel(dots, basis, scale, displacement, residual):
    order = [(i, k) for i in range(4) for k in range(i, 5)]
    gram = {}
    for value, (i, k) in zip(gathered(dots, len(order)), order):
        gram[i, k] = gram[k, i] = value
    zero = jnp.zeros((1, 1), jnp.float32)
    one = jnp.ones((1, 1), jnp.float32)
    res = [one]
    search = [one]
    disp = []
    res_dot = gram[0, 0]
    for iteration in range(4):
        image = [zero] * (iteration + 2)
        for i, value in enumerate(search):
            image[i] = image[i] + SHIFTS[i] * value
            image[i + 1] = image[i + 1] + value
        curve = zero
        for i, left in enumerate(search):
            inner = zero
            for k, right in enumerate(image):
                inner = inner + gram[i, k] * right
            curve = curve + left * inner
        step = res_dot / curve
        disp = [d + step * s for d, s in zip(disp + [zero], search)]
        res = [r - step * q for r, q in zip(res + [zero], image)]
        if iteration < 3:
            new_dot = zero
            for i, left in enumerate(res):
                inner = zero
                for k, right in enumerate(res):
                    inner = inner + gram[i, k] * right
                new_dot = new_dot + left * inner
            search = [r + new_dot / res_dot * s for r, s in zip(res, search + [zero])]
            res_dot = new_dot
    planes, rows, lanes = scale.shape
    disp = [jnp.broadcast_to(d, (8, lanes)) for d in disp]
    res = [jnp.broadcast_to(r, (8, lanes)) for r in res]

    def plane(p, carry):
        for r in range(0, rows, 8):
            inv = scale[p, r : r + 8]
            for c in range(3):
                ys = [basis[i, c, p, r : r + 8] for i in range(5)]
                first = disp[0] * ys[0]
                second = res[0] * ys[0]
                for i in range(1, 5):
                    second = second + res[i] * ys[i]
                    if i < 4:
                        first = first + disp[i] * ys[i]
                displacement[c, p, r : r + 8] = inv * first
                residual[c, p, r : r + 8] = second
        return carry

    lax.fori_loop(0, planes, plane, 0)


def call(kernel, outs, *args, scratch=()):
    f32 = lambda shape: jax.ShapeDtypeStruct(shape, jnp.float32)
    return pl.pallas_call(
        kernel,
        out_shape=tuple(f32(shape) for shape in outs),
        in_specs=[pl.BlockSpec(memory_space=pltpu.VMEM)] * len(args),
        out_specs=tuple(pl.BlockSpec(memory_space=pltpu.VMEM) for _ in outs),
        scratch_shapes=[pltpu.VMEM(shape, jnp.float32) for shape in scratch],
        compiler_params=pltpu.CompilerParams(vmem_limit_bytes=VMEM_LIMIT),
    )(*args)


def swapped(value, axis, first):
    count = lax.axis_size(axis)
    pairs = [(i, i + 1) for i in range(first, count - 1, 2)]
    if not pairs:
        return jnp.zeros_like(value)
    return lax.ppermute(value, axis, pairs + [(j, i) for i, j in pairs])


def paired_shards(density, fixed_mask, load_mask, load_values):
    planes, rows, lanes = density.shape
    devices = 1
    for axis in AXES:
        devices *= lax.axis_size(axis)
    grid = (rows * lax.axis_size("gy"), lanes * lax.axis_size("gz"))
    count = 2 * planes
    wide, tall = rows + 2 * FACE, rows + FACE
    face = (5 * planes, FACE, lanes)
    strips = (wide + 2 * tall, lanes)
    row = (devices, 1, lanes)
    fields, send_a, send_b = call(
        pack_kernel, ((5 * planes, rows, lanes), face, face), density, fixed_mask, load_mask, load_values
    )
    density_own, node_own, own, send_a, send_b = call(
        strip_kernel,
        ((planes, wide, lanes), (4 * planes, tall, lanes), strips, strips, strips),
        fields, swapped(send_a, "gy", 0), swapped(send_b, "gy", 1),
    )
    density_other = swapped(density_own, "gx", 0)
    node_other = swapped(node_own, "gx", 0)
    strip_own = own + swapped(send_a, "gz", 0) + swapped(send_b, "gz", 1)
    strip_other = swapped(strip_own, "gx", 0)
    window, first, strip_v, strip_g, dots = call(
        functools.partial(filter_kernel, grid),
        ((count, wide, lanes), (count, wide, lanes), (wide, lanes), (wide, lanes), row),
        density_own, density_other, strip_own, strip_other,
    )
    dots = lax.all_to_all(dots, AXES, 0, 0, tiled=True)
    table = element_table()
    diagonal = float(table[0, 0, 0, 0])
    plane = (tall, lanes)
    filtered, basis, scale, dots = call(
        functools.partial(solve_wrapped, grid, diagonal),
        ((planes, rows, lanes), (5, 3, planes, rows, lanes), (planes, rows, lanes), row),
        window, first, strip_v, strip_g, dots, node_own, node_other, strip_own, strip_other,
        scratch=(
            (5, 3, count) + plane,
            (count,) + plane, (count,) + plane, (count,) + plane,
            (6, count + 1, tall + 8, lanes), (12,) + plane, (12,) + plane, (6,) + plane, (6, tall + 8, lanes),
            (1,) + plane, plane, plane, (3,) + plane, (4, 3, tall + 8, lanes), (6,) + plane, (6, tall + 8, lanes),
            (4, 3) + plane,
        ),
    )
    dots = lax.all_to_all(dots, AXES, 0, 0, tiled=True)
    displacement, residual = call(combine_kernel, (load_values.shape, load_values.shape), dots, basis, scale)
    return (filtered, displacement, residual)


def solve_wrapped(
    grid, diagonal, window, first, strip_v, strip_g, filter_dots, node_own, node_other, strip_own, strip_other,
    filtered, fields, scale, dots, basis, modulus, inverse, free, pairs, kept, carried, near, far, *strip_scratch,
):
    solve_kernel(
        grid, diagonal, window, first, strip_v, strip_g, filter_dots, node_own, node_other, strip_own, strip_other,
        filtered, basis, scale, dots,
        modulus, inverse, free, fields, pairs, kept, carried, near, far, *strip_scratch,
    )


def shards(density, fixed_mask, load_mask, load_values):
    planes, rows, lanes = density.shape
    if lax.axis_size("gx") == 2 and 2 * planes * SW == lanes and lanes == 128 and rows % 8 == 0:
        return paired_shards(density, fixed_mask, load_mask, load_values)
    return general_shards(density, fixed_mask, load_mask, load_values)


def solution(mesh):
    return jax.shard_map(
        shards,
        mesh=mesh,
        in_specs=(
            P("gx", "gy", "gz"),
            P("gx", "gy", "gz"),
            P("gx", "gy", "gz"),
            P(None, "gx", "gy", "gz"),
        ),
        out_specs=(P("gx", "gy", "gz"), P(None, "gx", "gy", "gz"), P(None, "gx", "gy", "gz")),
        check_vma=False,
    )
```

```python
import functools

import jax
import jax.numpy as jnp
import numpy as np
from jax import lax
from jax.experimental import pallas as pl
from jax.experimental.pallas import tpu as pltpu
from jax.sharding import PartitionSpec as P

FILTER_ITERS = 2
SOLVE_ITERS = 4


MIN_MODULUS = 0.001
filter_weight = 0.75


def passed_along(value, axis, steps):
    count = lax.axis_size(axis)
    initial, last = (max(0, -steps), min(count, count - steps))
    return lax.ppermute(value, axis, [(source, source + steps) for source in range(initial, last)])


def padded_2(block, sides, width):
    for axis, dim in sides:
        count = lax.axis_size(axis)
        forward = [(i, i + 1) for i in range(count - 1)]
        backward = [(target, source) for source, target in forward]
        low = lax.ppermute(
            lax.slice_in_dim(block, block.shape[dim] - width, None, axis=dim), axis, forward
        )
        high = lax.ppermute(lax.slice_in_dim(block, 0, width, axis=dim), axis, backward)
        block = jnp.concatenate([low, block, high], axis=dim)
    return block


def element_table():
    poisson = 0.3
    lame_first = poisson / ((1.0 + poisson) * (1.0 - 2.0 * poisson))
    lame_shear = 1.0 / (2.0 * (1.0 + poisson))
    elastic = np.zeros((6, 6))
    elastic[:3, :3] = lame_first
    for index in range(3):
        elastic[index, index] += 2.0 * lame_shear
        elastic[index + 3, index + 3] = lame_shear
    gauss_value = 1.0 / np.sqrt(3.0)
    matrix = np.zeros((24, 24))
    for first in (-gauss_value, gauss_value):
        for second in (-gauss_value, gauss_value):
            for third in (-gauss_value, gauss_value):
                gauss_point = (first, second, third)
                strain = np.zeros((6, 24))
                for corner in range(8):
                    corner_signs = [
                        2 * (corner >> 2 & 1) - 1,
                        2 * (corner >> 1 & 1) - 1,
                        2 * (corner & 1) - 1,
                    ]
                    factors = [1.0 + corner_signs[d] * gauss_point[d] for d in range(3)]
                    slopes = [
                        corner_signs[d] * factors[(d + 1) % 3] * factors[(d + 2) % 3] / 4.0
                        for d in range(3)
                    ]
                    column = 3 * corner
                    strain[0, column] = slopes[0]
                    strain[1, column + 1] = slopes[1]
                    strain[2, column + 2] = slopes[2]
                    strain[3, column] = slopes[1]
                    strain[3, column + 1] = slopes[0]
                    strain[4, column + 1] = slopes[2]
                    strain[4, column + 2] = slopes[1]
                    strain[5, column] = slopes[2]
                    strain[5, column + 2] = slopes[0]
                matrix += strain.T @ elastic @ strain / 8.0
    return matrix.reshape(8, 3, 8, 3).transpose(0, 2, 1, 3)


def corner_offsets(corner):
    return (corner >> 2 & 1, corner >> 1 & 1, corner & 1)


def apply_stiffness(disp_pad, mod_pad, extent):
    stiffness = jnp.asarray(element_table(), jnp.float32)
    size_x, size_y, size_z = extent
    result = jnp.zeros((3, size_x, size_y, size_z), jnp.float32)
    for corner_a in range(8):
        offs_a = corner_offsets(corner_a)
        moduli_part = mod_pad[
            1 - offs_a[0] : 1 - offs_a[0] + size_x,
            1 - offs_a[1] : 1 - offs_a[1] + size_y,
            1 - offs_a[2] : 1 - offs_a[2] + size_z,
        ]
        inner_sum = jnp.zeros((3, size_x, size_y, size_z), jnp.float32)
        for corner_b in range(8):
            offs_b = corner_offsets(corner_b)
            start_x = 1 - offs_a[0] + offs_b[0]
            start_y = 1 - offs_a[1] + offs_b[1]
            start_z = 1 - offs_a[2] + offs_b[2]
            shifted = disp_pad[
                :,
                start_x : start_x + size_x,
                start_y : start_y + size_y,
                start_z : start_z + size_z,
            ]
            for comp in range(3):
                inner_sum = (
                    inner_sum
                    + stiffness[corner_a, corner_b, :, comp][:, None, None, None]
                    * shifted[comp][None]
                )
        result = result + moduli_part[None] * inner_sum
    return result


def jacobi_diagonal(mod_pad, extent):
    stiffness = jnp.asarray(element_table(), jnp.float32)
    size_x, size_y, size_z = extent
    diagonal = jnp.zeros((3, size_x, size_y, size_z), jnp.float32)
    for corner_a in range(8):
        offs_a = corner_offsets(corner_a)
        moduli_part = mod_pad[
            1 - offs_a[0] : 1 - offs_a[0] + size_x,
            1 - offs_a[1] : 1 - offs_a[1] + size_y,
            1 - offs_a[2] : 1 - offs_a[2] + size_z,
        ]
        block_diag = jnp.stack([stiffness[corner_a, corner_a, comp, comp] for comp in range(3)])
        diagonal = diagonal + moduli_part[None] * block_diag[:, None, None, None]
    return diagonal


def face_sum(padded):
    beside = padded[2:, 1:-1, 1:-1] + padded[:-2, 1:-1, 1:-1]
    beside = beside + padded[1:-1, 2:, 1:-1] + padded[1:-1, :-2, 1:-1]
    return beside + padded[1:-1, 1:-1, 2:] + padded[1:-1, 1:-1, :-2]


def edge_count(global_index, total):
    return (global_index > 0).astype(jnp.float32) + (global_index < total - 1).astype(jnp.float32)


def neighbour_counts(extent):
    size_x, size_y, size_z = extent
    index_x = lax.axis_index("gx") * size_x + jnp.arange(size_x, dtype=jnp.int32)
    index_y = lax.axis_index("gy") * size_y + jnp.arange(size_y, dtype=jnp.int32)
    index_z = lax.axis_index("gz") * size_z + jnp.arange(size_z, dtype=jnp.int32)
    count_x = edge_count(index_x, size_x * lax.axis_size("gx"))
    count_y = edge_count(index_y, size_y * lax.axis_size("gy"))
    count_z = edge_count(index_z, size_z * lax.axis_size("gz"))
    return count_x[:, None, None] + count_y[None, :, None] + count_z[None, None, :]


def lower_moduli(moduli):
    rim_x = passed_along(moduli[-1:], "gx", 1)
    extended = jnp.concatenate([rim_x, moduli], axis=0)
    rim_y = passed_along(extended[:, -1:], "gy", 1)
    extended = jnp.concatenate([rim_y, extended], axis=1)
    rim_z = passed_along(extended[:, :, -1:], "gz", 1)
    return jnp.concatenate([rim_z, extended], axis=2)


def displacement_halo(field):
    return padded_2(field, (("gx", 1), ("gy", 2), ("gz", 3)), 1)


def residual_dot(first, second):
    return lax.psum(jnp.sum(first * second), ("gx", "gy", "gz"))


def curvature_dot(first, second):
    return lax.psum(jnp.sum(first * second), ("gx", "gy", "gz"))


def conjugate(operator, precond, force, iters):
    iterate = jnp.zeros_like(force)
    residual = force
    search = precond(residual)
    direction = search
    res_dot = residual_dot(residual, search)
    for iteration in range(iters):
        image = operator(direction)
        step_size = res_dot / curvature_dot(direction, image)
        iterate = iterate + step_size * direction
        residual = residual - step_size * image
        if iteration + 1 < iters:
            search = precond(residual)
            new_dot = residual_dot(residual, search)
            direction = search + new_dot / res_dot * direction
            res_dot = new_dot
    return (iterate, residual)


def general_shards(density, fixed_mask, load_mask, load_values):
    extent = density.shape
    counts = neighbour_counts(extent)

    def filter_apply(field):
        padded = padded_2(field, (("gx", 0), ("gy", 1), ("gz", 2)), 1)
        return field + filter_weight * (counts * field - face_sum(padded))

    def identity(field):
        return field

    filtered, unused = conjugate(filter_apply, identity, density, FILTER_ITERS)
    moduli = MIN_MODULUS + (1.0 - MIN_MODULUS) * filtered * filtered * jnp.abs(filtered)
    mod_pad = lower_moduli(moduli)
    free_nodes = (1 - fixed_mask).astype(jnp.float32)
    force = free_nodes[None] * load_mask.astype(jnp.float32)[None] * load_values
    inverse_diag = free_nodes[None] / jacobi_diagonal(mod_pad, extent)

    def elastic_apply(field):
        return free_nodes[None] * apply_stiffness(displacement_halo(field), mod_pad, extent)

    def jacobi(field):
        return inverse_diag * field

    displacement, residual = conjugate(elastic_apply, jacobi, force, SOLVE_ITERS)
    return (filtered, displacement, residual)


HALO = 4
SW = 16
FACE = 8
PARTS = 8
AXES = ("gx", "gy", "gz")
SHIFTS = (1.2, 0.4, 2.0, 0.8)
VMEM_LIMIT = 24 * 1024 * 1024
POISSON = 0.3
LAME = POISSON / ((1.0 + POISSON) * (1.0 - 2.0 * POISSON))
SHEAR = 1.0 / (2.0 * (1.0 + POISSON))
AXIAL = LAME + 2.0 * SHEAR
MODES = [(a, b, g) for a in range(2) for b in range(2) for g in range(2)]


def lanes_of(shape):
    return lax.broadcasted_iota(jnp.int32, shape, len(shape) - 1)


def rows_of(shape):
    return lax.broadcasted_iota(jnp.int32, shape, len(shape) - 2)


def turned(value, shift, axis):
    size = value.shape[axis]
    if isinstance(shift, int):
        shift = shift % size
        if shift == 0:
            return value
    else:
        shift = lax.rem(shift + 4 * size, size)
    return pltpu.roll(value, shift, axis)


def either(flag, first, second):
    return jnp.where(jnp.full(first.shape, flag, jnp.int32) == 0, first, second)


def face_kernel(density, fixed, load_mask, load_values, send_a, send_b, bare_a, bare_b, d, f, m, v, done):
    planes, rows, _ = density.shape
    copies = []
    for side, at in ((0, 0), (1, rows - FACE)):
        for source, target in ((density, d), (fixed, f), (load_mask, m)):
            copies.append((source.at[:, at : at + FACE, :], target.at[side]))
        copies.append((load_values.at[:, :, at : at + FACE, :], v.at[side]))
    copies = [pltpu.make_async_copy(src, dst, done.at[n]) for n, (src, dst) in enumerate(copies)]
    for copy in copies:
        copy.start()
    for copy in copies:
        copy.wait()
    odd = lax.rem(lax.axis_index("gy"), 2)
    for send, bare, side in ((send_a, bare_a, 1 - odd), (send_b, bare_b, odd)):
        free = (1 - f[side]).astype(jnp.float32)
        loaded = free * m[side].astype(jnp.float32)
        send[:planes] = d[side]
        bare[...] = d[side]
        send[planes : 2 * planes] = free
        for c in range(3):
            send[(2 + c) * planes : (3 + c) * planes] = loaded * v[side, c]


def strip_kernel(
    density, other, fixed, load_mask, load_values, from_a, from_b, bare_a, bare_b, window, nodes, strips
):
    planes, rows, lanes = density.shape
    wide, tall = rows + 2 * FACE, rows + FACE
    mine = lax.axis_index("gx") * planes
    odd_y = lax.rem(lax.axis_index("gy"), 2)
    row = rows_of((FACE, lanes))
    for source, a, b, at in ((density, from_a, from_b, mine), (other, bare_a, bare_b, planes - mine)):
        for p in range(planes):
            window[at + p, :rows] = source[p]
            window[at + p, rows : rows + FACE] = either(odd_y, a[p], b[p])
            window[at + p, rows + FACE :] = either(odd_y, b[p], a[p])
    lane = lanes_of((wide, lanes))
    packed = jnp.zeros((wide, lanes), jnp.float32)
    for p in range(2 * planes):
        packed = jnp.where(lane // SW == p, turned(window[p], SW * p + 8, 1), packed)
    strips[:wide] = packed
    for p in range(planes):
        free = (1 - fixed[p]).astype(jnp.float32)
        loaded = free * load_mask[p].astype(jnp.float32)
        nodes[p, :rows] = free
        for c in range(3):
            nodes[(1 + c) * planes + p, :rows] = loaded * load_values[c, p]
    for q in range(4 * planes):
        above = either(odd_y, from_a[planes + q], from_b[planes + q])
        below = either(odd_y, from_b[planes + q], from_a[planes + q])
        nodes[q, rows:] = jnp.where(row < HALO, above, below)
    lane = lanes_of((tall, lanes))
    for pair in range(2):
        packed = jnp.zeros((tall, lanes), jnp.float32)
        for q in range(2 * planes):
            value = nodes[2 * planes * pair + q]
            packed = jnp.where(lane // SW == q, turned(value, SW * q + 12, 1), packed)
        strips[wide + pair * tall : wide + (pair + 1) * tall] = packed


def filter_kernel(grid, window, strips, from_a, from_b, first, strip_v, strip_g, node_strips, dots):
    count, wide, lanes = window.shape
    rows = wide - 2 * FACE
    planes = count // 2
    total_y, total_z = grid
    mine = lax.axis_index("gx") * planes
    odd_z = lax.rem(lax.axis_index("gz"), 2)
    base_y = lax.axis_index("gy") * rows
    base_z = lax.axis_index("gz") * lanes
    shape = (wide, lanes)
    lane = lanes_of(shape)
    row = rows_of(shape)
    place = lax.rem(lane, SW)
    strip_v[...] = jnp.where(
        place < 8, either(odd_z, from_b[:wide], from_a[:wide]), either(odd_z, from_a[:wide], from_b[:wide])
    )
    at_y = base_y + jnp.where(row < rows + FACE, row, row - wide)
    pass_y = ((at_y >= 0) & (at_y < total_y - 1)).astype(jnp.float32)
    pass_z = (base_z + lane < total_z - 1).astype(jnp.float32)
    back_z = (base_z + lane > 0).astype(jnp.float32)
    at_strip = base_z + jnp.where(place < 8, place - 8, lanes - 8 + place)
    strip_pass = ((at_strip >= 0) & (at_strip < total_z - 1)).astype(jnp.float32)
    strip_back = ((at_strip >= 1) & (at_strip < total_z)).astype(jnp.float32)

    def along_y(value):
        ahead = (turned(value, -1, 0) - value) * pass_y
        return turned(ahead, 1, 0) - ahead

    def laplace(source, strip, p):
        value = source[p]
        result = (value - source[jnp.minimum(p + 1, count - 1)]) + (value - source[jnp.maximum(p - 1, 0)])
        result = result + along_y(value)
        side = strip[...]
        ahead = jnp.where(lane == lanes - 1, turned(side, lanes - 1 - (SW * p + 8), 1), turned(value, -1, 1))
        behind = jnp.where(lane == 0, turned(side, 0 - (SW * p + 7), 1), turned(value, 1, 1))
        result = result + (value - ahead) * pass_z + (value - behind) * back_z
        return filter_weight * result

    def first_plane(p, carry):
        first[p] = laplace(window, strip_v, p)
        return carry

    lax.fori_loop(0, count, first_plane, 0)
    value = strip_v[...]
    edge_low = jnp.zeros(shape, jnp.float32)
    edge_high = edge_low
    for p in range(count):
        edge_low = jnp.where(lane == SW * p + 7, turned(window[p], SW * p + 7, 1), edge_low)
        edge_high = jnp.where(lane == SW * p + 8, turned(window[p], SW * p + 8 - (lanes - 1), 1), edge_high)
    ahead = jnp.where(place == 7, edge_low, turned(value, -1, 1))
    behind = jnp.where(place == 8, edge_high, turned(value, 1, 1))
    result = along_y(value) + (value - ahead) * strip_pass + (value - behind) * strip_back
    ahead = jnp.where(lane < lanes - SW, turned(value, -SW, 1) - value, 0.0)
    result = result + turned(ahead, SW, 1) - ahead
    strip_g[...] = filter_weight * result

    def add_dots(p, sums):
        plane = mine + p
        w = window[plane][:rows]
        g = first[plane][:rows]
        gg = laplace(first, strip_g, plane)[:rows]
        terms = (w * w, w * g, g * g, g * gg)
        return tuple(
            s + jnp.sum(t.reshape(rows // 8, 8, lanes), axis=0) for s, t in zip(sums, terms)
        )

    zero = jnp.zeros((8, lanes), jnp.float32)
    spread(lax.fori_loop(0, planes, add_dots, (zero,) * 4), dots)
    half = node_strips.shape[0] // 2
    place = lax.rem(lanes_of((half, lanes)), SW)
    node_strips[:half] = jnp.where(place < 12, strips[wide:], either(odd_z, from_a[wide:], from_b[wide:]))
    node_strips[half:] = either(odd_z, from_b[wide:], from_a[wide:])


def spread(sums, dots):
    lanes = dots.shape[-1]
    lane = lanes_of((1, lanes))
    line = jnp.zeros((1, lanes), jnp.float32)
    for k, value in enumerate(sums):
        value = jnp.sum(jnp.sum(value, axis=0, keepdims=True), axis=1, keepdims=True)
        line = jnp.where(lane == k, value, line)
    for k in range(dots.shape[0]):
        dots[k] = line


def gathered(dots, count):
    line = jnp.sum(dots[...], axis=0)
    lane = lanes_of(line.shape)
    return [
        jnp.sum(jnp.where(lane == k, line, 0.0), axis=1, keepdims=True) for k in range(count)
    ]


def element_forces(u, modulus):
    shear = modulus * (SHEAR / 16.0)
    shear_3 = modulus * (SHEAR / 48.0)
    twist = modulus * ((AXIAL + 2.0 * SHEAR) / 144.0)
    normal = modulus * (2.0 * SHEAR / 16.0)
    paired = modulus * ((AXIAL + SHEAR) / 48.0)
    x, y, z = u
    f = [{}, {}, {}]
    trace = (x[1, 0, 0] + y[0, 1, 0] + z[0, 0, 1]) * (LAME / (2.0 * SHEAR))
    f[0][1, 0, 0] = (trace + x[1, 0, 0]) * normal
    f[1][0, 1, 0] = (trace + y[0, 1, 0]) * normal
    f[2][0, 0, 1] = (trace + z[0, 0, 1]) * normal
    ratio = LAME / (AXIAL + SHEAR)
    for (c, m), (d, n) in (
        ((0, (1, 1, 0)), (2, (0, 1, 1))),
        ((1, (1, 1, 0)), (2, (1, 0, 1))),
        ((0, (1, 0, 1)), (1, (0, 1, 1))),
    ):
        f[c][m] = (u[c][m] + ratio * u[d][n]) * paired
        f[d][n] = (u[d][n] + ratio * u[c][m]) * paired
    for (c, m), (d, n) in (
        ((0, (0, 1, 0)), (1, (1, 0, 0))),
        ((1, (0, 0, 1)), (2, (0, 1, 0))),
        ((0, (0, 0, 1)), (2, (1, 0, 0))),
    ):
        f[c][m] = f[d][n] = (u[c][m] + u[d][n]) * shear
    three = ((0, (0, 1, 1)), (1, (1, 0, 1)), (2, (1, 1, 0)))
    both = x[0, 1, 1] + y[1, 0, 1] + z[1, 1, 0]
    for c, m in three:
        f[c][m] = (both + u[c][m]) * shear_3
    for c in range(3):
        f[c][1, 1, 1] = u[c][1, 1, 1] * twist
    return f


def solve_kernel(
    grid, diagonal, window, first, strip_v, strip_g, filter_dots, node_own, node_other, strip_own, strip_other,
    filtered, fields, strip_fields, scale, strip_scale, dots,
    basis, modulus, inverse, free, pairs, kept, carried, near, far,
    s_basis, s_modulus, s_inverse, s_free, s_pairs, s_near, s_far, s_part, s_disp,
):
    count, wide, lanes = window.shape
    rows = wide - 2 * FACE
    tall = rows + FACE
    tiles = tall // 8
    planes = count // 2
    total_y, total_z = grid
    gx = lax.axis_index("gx")
    base_y = lax.axis_index("gy") * rows
    base_z = lax.axis_index("gz") * lanes
    mine = gx * planes

    a, b, c, e = gathered(filter_dots, 4)
    step = a / (a + b)
    beta = step * step * (c - b * b / a) / a
    to_v = step * b / a + beta
    to_g = -step
    bottom = to_v * to_v * (a + b) + 2.0 * to_v * to_g * (b + c) + to_g * to_g * (c + e)
    second = beta * a / bottom
    weight_v = step + second * to_v
    weight_g = second * to_g

    shape = (wide, lanes)
    lane = lanes_of(shape)
    row = rows_of(shape)
    at_y = base_y + jnp.where(row < rows + FACE, row, row - wide)
    inside_y = (at_y >= 0) & (at_y < total_y)
    place = lax.rem(lane, SW)
    at_strip = base_z + jnp.where(place < 8, place - 8, lanes - 8 + place)
    inside_strip = inside_y & (at_strip >= 0) & (at_strip < total_z)
    small = rows_of((8, lanes))

    def folded(value):
        tail = jnp.where(small < HALO, value[rows : rows + 8], value[rows + 8 :])
        return value[:rows], tail

    def moduli_of(v, g):
        value = weight_v * v + weight_g * g
        return MIN_MODULUS + (1.0 - MIN_MODULUS) * value * value * jnp.abs(value)

    def inverted(total, open_nodes):
        return jnp.where(total > 0.0, open_nodes / jnp.where(total > 0.0, diagonal * total, 1.0), 0.0)

    tall_lane = lanes_of((tall, lanes))
    for source, strip, at in ((node_own, strip_own, mine), (node_other, strip_other, planes - mine)):
        for f in range(4):
            for p in range(planes):
                q = (f % 2) * planes + p
                begin = (2 + f // 2) * tall
                before = turned(strip[begin : begin + tall], lanes - HALO - (SW * q + 8), 1)
                value = jnp.where(tall_lane < lanes - HALO, source[f * planes + p], before)
                if f == 0:
                    free[at + p] = value
                else:
                    basis[0, f - 1, at + p] = value
    half = lanes // 2
    left = tall_lane < half
    for pair in range(2):
        at = pair * tall
        lower = either(gx, strip_own[at : at + tall], strip_other[at : at + tall])
        upper = either(gx, strip_other[at : at + tall], strip_own[at : at + tall])
        one = jnp.where(left, lower, turned(upper, half, 1))
        two = jnp.where(left, turned(lower, half, 1), upper)
        for k, value in ((2 * pair, one), (2 * pair + 1, two)):
            if k == 0:
                s_free[...] = value
            else:
                s_basis[0, k - 1] = value

    side = jnp.where(inside_strip, moduli_of(strip_v[...], strip_g[...]), 0.0)
    s_mod = turned(side, 4, 1)
    s_back = jnp.zeros(shape, jnp.float32)
    previous = jnp.zeros(shape, jnp.float32)
    for p in range(count):
        mod = jnp.where(inside_y, moduli_of(window[p], first[p]), 0.0)
        before = turned(side, lanes - HALO - (SW * p + 4), 1)
        across = jnp.where(lane >= lanes - HALO, before, mod)
        head, tail = folded(across)
        modulus[p, :rows] = head
        modulus[p, rows:] = tail
        across = across + turned(jnp.where(lane >= lanes - HALO - 1, before, mod), 1, 1)
        across = across + turned(across, 1, 0)
        head, tail = folded(across + previous)
        previous = across
        inverse[p, :rows] = inverted(head, free[p, :rows])
        inverse[p, rows:] = inverted(tail, free[p, rows:])
        inside = (lane // SW == p) & (place < 12)
        s_mod = jnp.where(inside, turned(mod, SW * p + 12, 1), s_mod)
        s_back = jnp.where(inside, turned(mod, SW * p + 13, 1), s_back)
    for p in range(planes):
        filtered[p] = (weight_v * window[mine + p] + weight_g * first[mine + p])[:rows]
    head, tail = folded(s_mod)
    s_modulus[:rows] = head
    s_modulus[rows:] = tail
    across = s_mod + jnp.where(place < 12, s_back, turned(s_mod, 1, 1))
    across = across + turned(across, 1, 0)
    across = across + jnp.where(lane < SW, 0.0, turned(across, SW, 1))
    head, tail = folded(across)
    s_inverse[:rows] = inverted(head, s_free[:rows])
    s_inverse[rows:] = inverted(tail, s_free[rows:])

    lane = lanes_of((8, lanes))
    last_plane = lane >= lanes - SW
    first_plane = lane < SW
    starts = range(0, tall, 8)

    def strip_pairs():
        for c in range(3):
            for r in starts:
                value = s_disp[c, r : r + 8]
                ahead = turned(value, -1, 1)
                s_part[2 * c, r : r + 8] = value + ahead
                s_part[2 * c + 1, r : r + 8] = ahead - value
        for k in range(6):
            for r in starts:
                value = s_part[k, r : r + 8]
                beside = jnp.where(last_plane, 0.0, turned(value, -SW, 1))
                s_pairs[2 * k, r : r + 8] = value + beside
                s_pairs[2 * k + 1, r : r + 8] = beside - value
            for n in (2 * k, 2 * k + 1):
                s_pairs[n, tall : tall + 1] = s_pairs[n, 0:1]

    for c in range(3):
        s_disp[c] = s_inverse[...] * s_basis[0, c]
    strip_pairs()
    for j in range(4):
        for r in starts:
            u = []
            for c in range(3):
                modes = {}
                for g in range(2):
                    for alpha in range(2):
                        k = 2 * (2 * c + g) + alpha
                        now = s_pairs[k, r : r + 8]
                        after = s_pairs[k, r + 1 : r + 9]
                        if (alpha, g) != (0, 0):
                            modes[alpha, 0, g] = now + after
                        modes[alpha, 1, g] = after - now
                u.append(modes)
            f = element_forces(u, s_modulus[r : r + 8])
            for c in range(3):
                for g in range(2):
                    for alpha in range(2):
                        k = 2 * (2 * c + g) + alpha
                        diff = f[c][alpha, 1, g]
                        if (alpha, g) == (0, 0):
                            s_near[k, r : r + 8] = -diff
                            s_far[k, r + 8 : r + 16] = diff
                        else:
                            total = f[c][alpha, 0, g]
                            s_near[k, r : r + 8] = total - diff
                            s_far[k, r + 8 : r + 16] = total + diff
        for k in range(12):
            s_far[k, 7:8] = s_far[k, tall + 7 : tall + 8]
        for k in range(6):
            for r in starts:
                total = s_near[2 * k, r : r + 8] + s_far[2 * k, r + 7 : r + 15]
                diff = s_near[2 * k + 1, r : r + 8] + s_far[2 * k + 1, r + 7 : r + 15]
                upper = jnp.where(first_plane, 0.0, turned(total + diff, SW, 1))
                s_part[k, r : r + 8] = (total - diff) + upper
        for c in range(3):
            for r in starts:
                total = s_part[2 * c, r : r + 8]
                diff = s_part[2 * c + 1, r : r + 8]
                out = (total - diff) + turned(total + diff, 1, 1)
                new = s_free[r : r + 8] * out - SHIFTS[j] * s_basis[j, c, r : r + 8]
                s_basis[j + 1, c, r : r + 8] = new
                if j < 3:
                    s_disp[c, r : r + 8] = s_inverse[r : r + 8] * new
        if j < 3:
            strip_pairs()

    def spread_z(c, p, r, disp):
        ahead = turned(disp, -1, 1)
        pairs[2 * c, p, r : r + 8] = disp + ahead
        pairs[2 * c + 1, p, r : r + 8] = ahead - disp

    def close_rows(p):
        for k in range(6):
            pairs[k, p, tall : tall + 1] = pairs[k, p, 0:1]

    for k in range(6):
        pairs[k, count] = jnp.zeros(pairs.shape[2:], jnp.float32)

    def start_plane(p, carry):
        for r in starts:
            for c in range(3):
                spread_z(c, p, r, inverse[p, r : r + 8] * basis[0, c, p, r : r + 8])
        close_rows(p)
        return carry

    lax.fori_loop(0, count, start_plane, 0)

    def along_rows(p, r):
        result = []
        for k in range(6):
            now = pairs[k, p, r : r + 8]
            after = pairs[k, p, r + 1 : r + 9]
            result.append((now + after, after - now))
        return result

    for j in range(4):
        low = gx * j
        high = count - 1 - j + gx * (j + 1)
        for r in starts:
            for k, both in enumerate(along_rows(low, r)):
                for beta_ in range(2):
                    kept[2 * k + beta_, r : r + 8] = both[beta_]
                    carried[2 * k + beta_, r : r + 8] = jnp.zeros((8, lanes), jnp.float32)

        def layer(p, state, j=j):
            for r in starts:
                upper_rows = along_rows(p + 1, r)
                u = []
                for c in range(3):
                    modes = {}
                    for g in range(2):
                        for beta_ in range(2):
                            k = 2 * (2 * c + g) + beta_
                            now = kept[k, r : r + 8]
                            above = upper_rows[2 * c + g][beta_]
                            if (beta_, g) != (0, 0):
                                modes[0, beta_, g] = now + above
                            modes[1, beta_, g] = above - now
                            kept[k, r : r + 8] = above
                    u.append(modes)
                f = element_forces(u, modulus[p, r : r + 8])
                for c in range(3):
                    for g in range(2):
                        t_beta = []
                        for beta_ in range(2):
                            k = 2 * (2 * c + g) + beta_
                            diff = f[c][1, beta_, g]
                            before = carried[k, r : r + 8]
                            if (beta_, g) == (0, 0):
                                t_beta.append(before - diff)
                                carried[k, r : r + 8] = diff
                            else:
                                total = f[c][0, beta_, g]
                                t_beta.append(before + (total - diff))
                                carried[k, r : r + 8] = total + diff
                        near[2 * c + g, r : r + 8] = t_beta[0] - t_beta[1]
                        far[2 * c + g, r + 8 : r + 16] = t_beta[0] + t_beta[1]
            for k in range(6):
                far[k, 7:8] = far[k, tall + 7 : tall + 8]
            for r in starts:
                open_nodes = free[p, r : r + 8]
                inv = inverse[p, r : r + 8]
                for c in range(3):
                    total = near[2 * c, r : r + 8] + far[2 * c, r + 7 : r + 15]
                    diff = near[2 * c + 1, r : r + 8] + far[2 * c + 1, r + 7 : r + 15]
                    out = (total - diff) + turned(total + diff, 1, 1)
                    new = open_nodes * out - SHIFTS[j] * basis[j, c, p, r : r + 8]
                    basis[j + 1, c, p, r : r + 8] = new
                    if j < 3:
                        spread_z(c, p, r, inv * new)
            if j < 3:
                close_rows(p)
            return state

        lax.fori_loop(low, high, layer, 0)

    order = [(i, k) for i in range(4) for k in range(i, 5)]
    zero = jnp.zeros((8, lanes), jnp.float32)

    def add_dots(p, sums):
        plane = mine + p
        sums = list(sums)
        for r in range(0, rows, 8):
            inv = inverse[plane, r : r + 8]
            scale[p, r : r + 8] = inv
            for c in range(3):
                ys = [basis[i, c, plane, r : r + 8] for i in range(5)]
                ws = [inv * y for y in ys[:4]]
                for i in range(5):
                    fields[i, c, p, r : r + 8] = ys[i]
                for n, (i, k) in enumerate(order):
                    sums[n] = sums[n] + ws[i] * ys[k]
        return tuple(sums)

    main = lax.fori_loop(0, planes, add_dots, (zero,) * len(order))
    extra = [zero] * len(order)
    for r in range(0, rows, 8):
        inv = s_inverse[r : r + 8]
        strip_scale[r : r + 8] = inv
        for c in range(3):
            ys = [s_basis[i, c, r : r + 8] for i in range(5)]
            ws = [inv * y for y in ys[:4]]
            for i in range(5):
                strip_fields[i, c, r : r + 8] = ys[i]
            for n, (i, k) in enumerate(order):
                extra[n] = extra[n] + ws[i] * ys[k]
    place = lax.rem(lane, SW)
    own_lanes = (place >= 4) & (place < 12) & (lane // (SW * planes) == gx)
    sums = [
        jnp.where(lane < lanes - 8, value, 0.0) + jnp.where(own_lanes, more, 0.0) for value, more in zip(main, extra)
    ]
    spread(sums, dots)


def combine_kernel(dots, basis, strips, scale, strip_scale, displacement, residual, ends):
    order = [(i, k) for i in range(4) for k in range(i, 5)]
    gram = {}
    for value, (i, k) in zip(gathered(dots, len(order)), order):
        gram[i, k] = gram[k, i] = value
    zero = jnp.zeros((1, 1), jnp.float32)
    one = jnp.ones((1, 1), jnp.float32)
    res = [one]
    search = [one]
    disp = []
    res_dot = gram[0, 0]
    for iteration in range(4):
        image = [zero] * (iteration + 2)
        for i, value in enumerate(search):
            image[i] = image[i] + SHIFTS[i] * value
            image[i + 1] = image[i + 1] + value
        curve = zero
        for i, left in enumerate(search):
            inner = zero
            for k, right in enumerate(image):
                inner = inner + gram[i, k] * right
            curve = curve + left * inner
        step = res_dot / curve
        disp = [d + step * s for d, s in zip(disp + [zero], search)]
        res = [r - step * q for r, q in zip(res + [zero], image)]
        if iteration < 3:
            new_dot = zero
            for i, left in enumerate(res):
                inner = zero
                for k, right in enumerate(res):
                    inner = inner + gram[i, k] * right
                new_dot = new_dot + left * inner
            search = [r + new_dot / res_dot * s for r, s in zip(res, search + [zero])]
            res_dot = new_dot
    planes, rows, lanes = scale.shape
    disp = [jnp.broadcast_to(d, (8, lanes)) for d in disp]
    res = [jnp.broadcast_to(r, (8, lanes)) for r in res]

    def combined(ys, inv):
        first = disp[0] * ys[0]
        second = res[0] * ys[0]
        for i in range(1, 5):
            second = second + res[i] * ys[i]
            if i < 4:
                first = first + disp[i] * ys[i]
        return inv * first, second

    for r in range(0, rows, 8):
        for c in range(3):
            both = combined([strips[i, c, r : r + 8] for i in range(5)], strip_scale[r : r + 8])
            ends[c, r : r + 8], ends[3 + c, r : r + 8] = both
    mine = lax.axis_index("gx") * planes
    lane = lanes_of((8, lanes))

    def plane(p, carry):
        shift = lanes - 8 - (SW * (mine + p) + 4)
        for r in range(0, rows, 8):
            inv = scale[p, r : r + 8]
            for c in range(3):
                both = combined([basis[i, c, p, r : r + 8] for i in range(5)], inv)
                for n, out in enumerate((displacement, residual)):
                    end = turned(ends[3 * n + c, r : r + 8], shift, 1)
                    out[c, p, r : r + 8] = jnp.where(lane < lanes - 8, both[n], end)
        return carry

    lax.fori_loop(0, planes, plane, 0)


def call(kernel, outs, *args, scratch=(), space=pltpu.VMEM):
    return pl.pallas_call(
        kernel,
        out_shape=tuple(jax.ShapeDtypeStruct(shape, jnp.float32) for shape in outs),
        in_specs=[pl.BlockSpec(memory_space=space)] * len(args),
        out_specs=tuple(pl.BlockSpec(memory_space=pltpu.VMEM) for _ in outs),
        scratch_shapes=list(scratch),
        compiler_params=pltpu.CompilerParams(vmem_limit_bytes=VMEM_LIMIT),
    )(*args)


def swapped(value, axis, first, across=False):
    count = lax.axis_size(axis)
    pairs = [(i, i + 1) for i in range(first, count - 1, 2)]
    pairs = pairs + [(j, i) for i, j in pairs]
    if not pairs:
        return jnp.zeros_like(value)
    if not across:
        return lax.ppermute(value, axis, pairs)
    return lax.ppermute(value, ("gx", axis), [(x * count + i, (1 - x) * count + j) for x in range(2) for i, j in pairs])


def paired_shards(density, fixed_mask, load_mask, load_values):
    planes, rows, lanes = density.shape
    devices = 1
    for axis in AXES:
        devices *= lax.axis_size(axis)
    grid = (rows * lax.axis_size("gy"), lanes * lax.axis_size("gz"))
    count = 2 * planes
    wide, tall = rows + 2 * FACE, rows + FACE
    face, bare = (5 * planes, FACE, lanes), (planes, FACE, lanes)
    row = (devices, 1, lanes)
    f32, i32 = jnp.float32, jnp.int32
    density_other = swapped(density, "gx", 0)
    send_a, send_b, bare_a, bare_b = call(
        face_kernel, (face, face, bare, bare), density, fixed_mask, load_mask, load_values, space=pl.ANY,
        scratch=(
            pltpu.VMEM((2,) + bare, f32), pltpu.VMEM((2,) + bare, i32), pltpu.VMEM((2,) + bare, i32),
            pltpu.VMEM((2, 3) + bare, f32), pltpu.SemaphoreType.DMA((8,)),
        ),
    )
    window, nodes, strips = call(
        strip_kernel,
        ((count, wide, lanes), (4 * planes, tall, lanes), (wide + 2 * tall, lanes)),
        density, density_other, fixed_mask, load_mask, load_values,
        swapped(send_a, "gy", 0), swapped(send_b, "gy", 1),
        swapped(bare_a, "gy", 0, True), swapped(bare_b, "gy", 1, True),
    )
    from_a, from_b = swapped(strips, "gz", 0), swapped(strips, "gz", 1)
    nodes_other = swapped(nodes, "gx", 0)
    first, strip_v, strip_g, node_strips, dots = call(
        functools.partial(filter_kernel, grid),
        ((count, wide, lanes), (wide, lanes), (wide, lanes), (4 * tall, lanes), row),
        window, strips, from_a, from_b,
    )
    strips_other = swapped(node_strips, "gx", 0)
    dots = lax.all_to_all(dots, AXES, 0, 0, tiled=True)
    diagonal = float(element_table()[0, 0, 0, 0])
    plane, taller = (tall, lanes), (tall + 8, lanes)
    many = (count,) + plane
    filtered, basis, strip_basis, scale, strip_scale, dots = call(
        functools.partial(solve_kernel, grid, diagonal),
        ((planes, rows, lanes), (5, 3, planes, rows, lanes), (5, 3, rows, lanes), (planes, rows, lanes), (rows, lanes), row),
        window, first, strip_v, strip_g, dots, nodes, nodes_other, node_strips, strips_other,
        scratch=[
            pltpu.VMEM(shape, f32)
            for shape in (
                (5, 3) + many, many, many, many, (6, count + 1) + taller, (12,) + plane, (12,) + plane, (6,) + plane, (6,) + taller,
                (5, 3) + plane, plane, plane, plane, (12,) + taller, (12,) + plane, (12,) + taller, (6,) + plane, (3,) + plane,
            )
        ],
    )
    dots = lax.all_to_all(dots, AXES, 0, 0, tiled=True)
    displacement, residual = call(
        combine_kernel, (load_values.shape, load_values.shape), dots, basis, strip_basis, scale, strip_scale,
        scratch=[pltpu.VMEM((6, rows, lanes), f32)],
    )
    return (filtered, displacement, residual)


def shards(density, fixed_mask, load_mask, load_values):
    planes, rows, lanes = density.shape
    if lax.axis_size("gx") == 2 and 2 * planes * SW == lanes and lanes == 128 and rows % 8 == 0:
        return paired_shards(density, fixed_mask, load_mask, load_values)
    return general_shards(density, fixed_mask, load_mask, load_values)


def solution(mesh):
    return jax.shard_map(
        shards,
        mesh=mesh,
        in_specs=(
            P("gx", "gy", "gz"),
            P("gx", "gy", "gz"),
            P("gx", "gy", "gz"),
            P(None, "gx", "gy", "gz"),
        ),
        out_specs=(P("gx", "gy", "gz"), P(None, "gx", "gy", "gz"), P(None, "gx", "gy", "gz")),
        check_vma=False,
    )
```

```python
import functools

import jax
import jax.numpy as jnp
import numpy as np
from jax import lax
from jax.experimental import pallas as pl
from jax.experimental.pallas import tpu as pltpu
from jax.sharding import PartitionSpec as P

FILTER_ITERS = 2
SOLVE_ITERS = 4


MIN_MODULUS = 0.001
filter_weight = 0.75


def passed_along(value, axis, steps):
    count = lax.axis_size(axis)
    initial, last = (max(0, -steps), min(count, count - steps))
    return lax.ppermute(value, axis, [(source, source + steps) for source in range(initial, last)])


def padded_2(block, sides, width):
    for axis, dim in sides:
        count = lax.axis_size(axis)
        forward = [(i, i + 1) for i in range(count - 1)]
        backward = [(target, source) for source, target in forward]
        low = lax.ppermute(
            lax.slice_in_dim(block, block.shape[dim] - width, None, axis=dim), axis, forward
        )
        high = lax.ppermute(lax.slice_in_dim(block, 0, width, axis=dim), axis, backward)
        block = jnp.concatenate([low, block, high], axis=dim)
    return block


def element_table():
    poisson = 0.3
    lame_first = poisson / ((1.0 + poisson) * (1.0 - 2.0 * poisson))
    lame_shear = 1.0 / (2.0 * (1.0 + poisson))
    elastic = np.zeros((6, 6))
    elastic[:3, :3] = lame_first
    for index in range(3):
        elastic[index, index] += 2.0 * lame_shear
        elastic[index + 3, index + 3] = lame_shear
    gauss_value = 1.0 / np.sqrt(3.0)
    matrix = np.zeros((24, 24))
    for first in (-gauss_value, gauss_value):
        for second in (-gauss_value, gauss_value):
            for third in (-gauss_value, gauss_value):
                gauss_point = (first, second, third)
                strain = np.zeros((6, 24))
                for corner in range(8):
                    corner_signs = [
                        2 * (corner >> 2 & 1) - 1,
                        2 * (corner >> 1 & 1) - 1,
                        2 * (corner & 1) - 1,
                    ]
                    factors = [1.0 + corner_signs[d] * gauss_point[d] for d in range(3)]
                    slopes = [
                        corner_signs[d] * factors[(d + 1) % 3] * factors[(d + 2) % 3] / 4.0
                        for d in range(3)
                    ]
                    column = 3 * corner
                    strain[0, column] = slopes[0]
                    strain[1, column + 1] = slopes[1]
                    strain[2, column + 2] = slopes[2]
                    strain[3, column] = slopes[1]
                    strain[3, column + 1] = slopes[0]
                    strain[4, column + 1] = slopes[2]
                    strain[4, column + 2] = slopes[1]
                    strain[5, column] = slopes[2]
                    strain[5, column + 2] = slopes[0]
                matrix += strain.T @ elastic @ strain / 8.0
    return matrix.reshape(8, 3, 8, 3).transpose(0, 2, 1, 3)


def corner_offsets(corner):
    return (corner >> 2 & 1, corner >> 1 & 1, corner & 1)


def apply_stiffness(disp_pad, mod_pad, extent):
    stiffness = jnp.asarray(element_table(), jnp.float32)
    size_x, size_y, size_z = extent
    result = jnp.zeros((3, size_x, size_y, size_z), jnp.float32)
    for corner_a in range(8):
        offs_a = corner_offsets(corner_a)
        moduli_part = mod_pad[
            1 - offs_a[0] : 1 - offs_a[0] + size_x,
            1 - offs_a[1] : 1 - offs_a[1] + size_y,
            1 - offs_a[2] : 1 - offs_a[2] + size_z,
        ]
        inner_sum = jnp.zeros((3, size_x, size_y, size_z), jnp.float32)
        for corner_b in range(8):
            offs_b = corner_offsets(corner_b)
            start_x = 1 - offs_a[0] + offs_b[0]
            start_y = 1 - offs_a[1] + offs_b[1]
            start_z = 1 - offs_a[2] + offs_b[2]
            shifted = disp_pad[
                :,
                start_x : start_x + size_x,
                start_y : start_y + size_y,
                start_z : start_z + size_z,
            ]
            for comp in range(3):
                inner_sum = (
                    inner_sum
                    + stiffness[corner_a, corner_b, :, comp][:, None, None, None]
                    * shifted[comp][None]
                )
        result = result + moduli_part[None] * inner_sum
    return result


def jacobi_diagonal(mod_pad, extent):
    stiffness = jnp.asarray(element_table(), jnp.float32)
    size_x, size_y, size_z = extent
    diagonal = jnp.zeros((3, size_x, size_y, size_z), jnp.float32)
    for corner_a in range(8):
        offs_a = corner_offsets(corner_a)
        moduli_part = mod_pad[
            1 - offs_a[0] : 1 - offs_a[0] + size_x,
            1 - offs_a[1] : 1 - offs_a[1] + size_y,
            1 - offs_a[2] : 1 - offs_a[2] + size_z,
        ]
        block_diag = jnp.stack([stiffness[corner_a, corner_a, comp, comp] for comp in range(3)])
        diagonal = diagonal + moduli_part[None] * block_diag[:, None, None, None]
    return diagonal


def face_sum(padded):
    beside = padded[2:, 1:-1, 1:-1] + padded[:-2, 1:-1, 1:-1]
    beside = beside + padded[1:-1, 2:, 1:-1] + padded[1:-1, :-2, 1:-1]
    return beside + padded[1:-1, 1:-1, 2:] + padded[1:-1, 1:-1, :-2]


def edge_count(global_index, total):
    return (global_index > 0).astype(jnp.float32) + (global_index < total - 1).astype(jnp.float32)


def neighbour_counts(extent):
    size_x, size_y, size_z = extent
    index_x = lax.axis_index("gx") * size_x + jnp.arange(size_x, dtype=jnp.int32)
    index_y = lax.axis_index("gy") * size_y + jnp.arange(size_y, dtype=jnp.int32)
    index_z = lax.axis_index("gz") * size_z + jnp.arange(size_z, dtype=jnp.int32)
    count_x = edge_count(index_x, size_x * lax.axis_size("gx"))
    count_y = edge_count(index_y, size_y * lax.axis_size("gy"))
    count_z = edge_count(index_z, size_z * lax.axis_size("gz"))
    return count_x[:, None, None] + count_y[None, :, None] + count_z[None, None, :]


def lower_moduli(moduli):
    rim_x = passed_along(moduli[-1:], "gx", 1)
    extended = jnp.concatenate([rim_x, moduli], axis=0)
    rim_y = passed_along(extended[:, -1:], "gy", 1)
    extended = jnp.concatenate([rim_y, extended], axis=1)
    rim_z = passed_along(extended[:, :, -1:], "gz", 1)
    return jnp.concatenate([rim_z, extended], axis=2)


def displacement_halo(field):
    return padded_2(field, (("gx", 1), ("gy", 2), ("gz", 3)), 1)


def residual_dot(first, second):
    return lax.psum(jnp.sum(first * second), ("gx", "gy", "gz"))


def curvature_dot(first, second):
    return lax.psum(jnp.sum(first * second), ("gx", "gy", "gz"))


def conjugate(operator, precond, force, iters):
    iterate = jnp.zeros_like(force)
    residual = force
    search = precond(residual)
    direction = search
    res_dot = residual_dot(residual, search)
    for iteration in range(iters):
        image = operator(direction)
        step_size = res_dot / curvature_dot(direction, image)
        iterate = iterate + step_size * direction
        residual = residual - step_size * image
        if iteration + 1 < iters:
            search = precond(residual)
            new_dot = residual_dot(residual, search)
            direction = search + new_dot / res_dot * direction
            res_dot = new_dot
    return (iterate, residual)


def general_shards(density, fixed_mask, load_mask, load_values):
    extent = density.shape
    counts = neighbour_counts(extent)

    def filter_apply(field):
        padded = padded_2(field, (("gx", 0), ("gy", 1), ("gz", 2)), 1)
        return field + filter_weight * (counts * field - face_sum(padded))

    def identity(field):
        return field

    filtered, unused = conjugate(filter_apply, identity, density, FILTER_ITERS)
    moduli = MIN_MODULUS + (1.0 - MIN_MODULUS) * filtered * filtered * jnp.abs(filtered)
    mod_pad = lower_moduli(moduli)
    free_nodes = (1 - fixed_mask).astype(jnp.float32)
    force = free_nodes[None] * load_mask.astype(jnp.float32)[None] * load_values
    inverse_diag = free_nodes[None] / jacobi_diagonal(mod_pad, extent)

    def elastic_apply(field):
        return free_nodes[None] * apply_stiffness(displacement_halo(field), mod_pad, extent)

    def jacobi(field):
        return inverse_diag * field

    displacement, residual = conjugate(elastic_apply, jacobi, force, SOLVE_ITERS)
    return (filtered, displacement, residual)


HALO = 4
SW = 16
FACE = 8
AXES = ("gx", "gy", "gz")
SHIFTS = (1.2, 0.4, 2.0, 0.8)
VMEM_LIMIT = 24 * 1024 * 1024
POISSON = 0.3
LAME = POISSON / ((1.0 + POISSON) * (1.0 - 2.0 * POISSON))
SHEAR = 1.0 / (2.0 * (1.0 + POISSON))
AXIAL = LAME + 2.0 * SHEAR
MODES = [(a, b, g) for a in range(2) for b in range(2) for g in range(2)]


def lanes_of(shape):
    return lax.broadcasted_iota(jnp.int32, shape, len(shape) - 1)


def rows_of(shape):
    return lax.broadcasted_iota(jnp.int32, shape, len(shape) - 2)


def turned(value, shift, axis):
    size = value.shape[axis]
    if isinstance(shift, int):
        shift = shift % size
        if shift == 0:
            return value
    else:
        shift = lax.rem(shift + 4 * size, size)
    return pltpu.roll(value, shift, axis)


def either(flag, first, second):
    return jnp.where(jnp.full(first.shape, flag, jnp.int32) == 0, first, second)


def node_kernel(density, fixed, load_mask, load_values, held, nodes):
    planes = density.shape[0]
    held[...] = density[...]
    for p in range(planes):
        free = (1 - fixed[p]).astype(jnp.float32)
        loaded = free * load_mask[p].astype(jnp.float32)
        nodes[p] = free
        for c in range(3):
            nodes[(1 + c) * planes + p] = loaded * load_values[c, p]


def face_kernel(density, other, nodes, send_a, send_b):
    planes, rows, lanes = density.shape
    half = 2 * planes
    gx = lax.axis_index("gx")
    odd = lax.rem(lax.axis_index("gy"), 2)
    top = rows - FACE
    row = rows_of((FACE, lanes))
    for p in range(planes):
        for source, at in ((density, gx * planes), (other, planes - gx * planes)):
            low, high = source[p, :FACE], source[p, top:]
            send_a[at + p] = either(odd, high, low)
            send_b[at + p] = either(odd, low, high)
    for q in range(half):
        low = jnp.where(row < HALO, nodes[q, :FACE], turned(nodes[q + half, :FACE], HALO, 0))
        high = jnp.where(row < HALO, turned(nodes[q + half, top:], HALO, 0), nodes[q, top:])
        send_a[half + q] = either(odd, high, low)
        send_b[half + q] = either(odd, low, high)


def strip_kernel(density, other, nodes, from_a, from_b, window, tails, strips):
    planes, rows, lanes = density.shape
    wide, tall = rows + 2 * FACE, rows + FACE
    half = 2 * planes
    mine = lax.axis_index("gx") * planes
    odd_y = lax.rem(lax.axis_index("gy"), 2)
    row = rows_of((FACE, lanes))
    for source, at in ((density, mine), (other, planes - mine)):
        for p in range(planes):
            window[at + p, :rows] = source[p]
    for p in range(half):
        window[p, rows : rows + FACE] = either(odd_y, from_a[p], from_b[p])
        window[p, rows + FACE :] = either(odd_y, from_b[p], from_a[p])
        above = either(odd_y, from_a[half + p], from_b[half + p])
        below = either(odd_y, from_b[half + p], from_a[half + p])
        tails[p] = jnp.where(row < HALO, above, below)
        tails[half + p] = jnp.where(row < HALO, turned(above, HALO, 0), turned(below, HALO, 0))
    for begin, end in ((0, rows), (rows, wide)):
        lane = lanes_of((end - begin, lanes))
        packed = jnp.zeros((end - begin, lanes), jnp.float32)
        for p in range(half):
            packed = jnp.where(lane // SW == p, turned(window[p, begin:end], SW * p + 8, 1), packed)
        strips[begin:end] = packed
    for pair in range(2):
        at = wide + pair * tall
        for source, size, begin in ((nodes, rows, at), (tails, FACE, at + rows)):
            lane = lanes_of((size, lanes))
            packed = jnp.zeros((size, lanes), jnp.float32)
            for q in range(half):
                packed = jnp.where(lane // SW == q, turned(source[half * pair + q], SW * q + 12, 1), packed)
            strips[begin : begin + size] = packed


def filter_kernel(grid, window, tails, strips, from_a, from_b, first, strip_v, strip_g, node_strips, dots):
    count, wide, lanes = window.shape
    rows = wide - 2 * FACE
    planes = count // 2
    total_y, total_z = grid
    mine = lax.axis_index("gx") * planes
    odd_z = lax.rem(lax.axis_index("gz"), 2)
    base_y = lax.axis_index("gy") * rows
    base_z = lax.axis_index("gz") * lanes
    shape = (wide, lanes)
    lane = lanes_of(shape)
    row = rows_of(shape)
    place = lax.rem(lane, SW)
    strip_v[...] = jnp.where(
        place < 8, either(odd_z, from_b[:wide], from_a[:wide]), either(odd_z, from_a[:wide], from_b[:wide])
    )
    at_y = base_y + jnp.where(row < rows + FACE, row, row - wide)
    pass_y = ((at_y >= 0) & (at_y < total_y - 1)).astype(jnp.float32)
    pass_z = (base_z + lane < total_z - 1).astype(jnp.float32)
    back_z = (base_z + lane > 0).astype(jnp.float32)
    at_strip = base_z + jnp.where(place < 8, place - 8, lanes - 8 + place)
    strip_pass = ((at_strip >= 0) & (at_strip < total_z - 1)).astype(jnp.float32)
    strip_back = ((at_strip >= 1) & (at_strip < total_z)).astype(jnp.float32)

    def along_y(value):
        ahead = (turned(value, -1, 0) - value) * pass_y
        return turned(ahead, 1, 0) - ahead

    def laplace(source, side, q, p, lower, upper):
        value = source[p]
        result = (value - source[upper]) + (value - source[lower])
        result = result + along_y(value)
        ahead = jnp.where(lane == lanes - 1, turned(side, lanes - 1 - (SW * q + 8), 1), turned(value, -1, 1))
        behind = jnp.where(lane == 0, turned(side, 0 - (SW * q + 7), 1), turned(value, 1, 1))
        result = result + (value - ahead) * pass_z + (value - behind) * back_z
        return filter_weight * result

    value = strip_v[...]
    for p in range(count):
        first[p] = laplace(window, value, p, p, max(p - 1, 0), min(p + 1, count - 1))
    edge_low = jnp.zeros(shape, jnp.float32)
    edge_high = edge_low
    for p in range(count):
        edge_low = jnp.where(lane == SW * p + 7, turned(window[p], SW * p + 7, 1), edge_low)
        edge_high = jnp.where(lane == SW * p + 8, turned(window[p], SW * p + 8 - (lanes - 1), 1), edge_high)
    ahead = jnp.where(place == 7, edge_low, turned(value, -1, 1))
    behind = jnp.where(place == 8, edge_high, turned(value, 1, 1))
    result = along_y(value) + (value - ahead) * strip_pass + (value - behind) * strip_back
    ahead = jnp.where(lane < lanes - SW, turned(value, -SW, 1) - value, 0.0)
    result = result + turned(ahead, SW, 1) - ahead
    strip_g[...] = filter_weight * result

    value = strip_g[...]
    value = either(mine, value, turned(value, lanes // 2, 1))
    sums = [jnp.zeros((8, lanes), jnp.float32)] * 4
    for p in range(planes):
        plane = mine + p
        w = window[plane][:rows]
        g = first[plane][:rows]
        gg = laplace(first, value, p, plane, jnp.maximum(plane - 1, 0), jnp.minimum(plane + 1, count - 1))[:rows]
        terms = (w * w, w * g, g * g, g * gg)
        sums = [s + jnp.sum(t.reshape(rows // 8, 8, lanes), axis=0) for s, t in zip(sums, terms)]
    spread(sums, dots)
    half = strips.shape[0] - wide
    place = lax.rem(lanes_of((half, lanes)), SW)
    node_strips[:half] = jnp.where(place < 12, strips[wide:], either(odd_z, from_a[wide:], from_b[wide:]))
    node_strips[half : 2 * half] = either(odd_z, from_b[wide:], from_a[wide:])
    for q in range(tails.shape[0]):
        node_strips[2 * half + FACE * q : 2 * half + FACE * (q + 1)] = tails[q]


def spread(sums, dots):
    lanes = dots.shape[-1]
    lane = lanes_of((1, lanes))
    line = jnp.zeros((1, lanes), jnp.float32)
    for k, value in enumerate(sums):
        value = jnp.sum(jnp.sum(value, axis=0, keepdims=True), axis=1, keepdims=True)
        line = jnp.where(lane == k, value, line)
    for k in range(dots.shape[0]):
        dots[k] = line


def gathered(dots, count):
    line = jnp.sum(dots[...], axis=0)
    lane = lanes_of(line.shape)
    return [
        jnp.sum(jnp.where(lane == k, line, 0.0), axis=1, keepdims=True) for k in range(count)
    ]


def element_forces(u, modulus):
    shear = modulus * (SHEAR / 16.0)
    shear_3 = modulus * (SHEAR / 48.0)
    twist = modulus * ((AXIAL + 2.0 * SHEAR) / 144.0)
    normal = modulus * (2.0 * SHEAR / 16.0)
    paired = modulus * ((AXIAL + SHEAR) / 48.0)
    x, y, z = u
    f = [{}, {}, {}]
    trace = (x[1, 0, 0] + y[0, 1, 0] + z[0, 0, 1]) * (LAME / (2.0 * SHEAR))
    f[0][1, 0, 0] = (trace + x[1, 0, 0]) * normal
    f[1][0, 1, 0] = (trace + y[0, 1, 0]) * normal
    f[2][0, 0, 1] = (trace + z[0, 0, 1]) * normal
    ratio = LAME / (AXIAL + SHEAR)
    for (c, m), (d, n) in (
        ((0, (1, 1, 0)), (2, (0, 1, 1))),
        ((1, (1, 1, 0)), (2, (1, 0, 1))),
        ((0, (1, 0, 1)), (1, (0, 1, 1))),
    ):
        f[c][m] = (u[c][m] + ratio * u[d][n]) * paired
        f[d][n] = (u[d][n] + ratio * u[c][m]) * paired
    for (c, m), (d, n) in (
        ((0, (0, 1, 0)), (1, (1, 0, 0))),
        ((1, (0, 0, 1)), (2, (0, 1, 0))),
        ((0, (0, 0, 1)), (2, (1, 0, 0))),
    ):
        f[c][m] = f[d][n] = (u[c][m] + u[d][n]) * shear
    three = ((0, (0, 1, 1)), (1, (1, 0, 1)), (2, (1, 1, 0)))
    both = x[0, 1, 1] + y[1, 0, 1] + z[1, 1, 0]
    for c, m in three:
        f[c][m] = (both + u[c][m]) * shear_3
    for c in range(3):
        f[c][1, 1, 1] = u[c][1, 1, 1] * twist
    return f


def solve_kernel(
    grid, diagonal, window, first, strip_v, strip_g, filter_dots, node_own, node_other, strip_own, strip_other,
    filtered, fields, strip_fields, scale, strip_scale, dots,
    basis_0, basis_1, basis_2, basis_3, basis_4, modulus, inverse, free, pairs, kept, carried, near, far,
    s_basis, s_modulus, s_inverse, s_free, s_pairs, s_near, s_far, s_part, s_disp,
):
    basis = (basis_0, basis_1, basis_2, basis_3, basis_4)
    count, wide, lanes = window.shape
    rows = wide - 2 * FACE
    tall = rows + FACE
    planes = count // 2
    total_y, total_z = grid
    gx = lax.axis_index("gx")
    base_y = lax.axis_index("gy") * rows
    base_z = lax.axis_index("gz") * lanes
    mine = gx * planes

    a, b, c, e = gathered(filter_dots, 4)
    step = a / (a + b)
    beta = step * step * (c - b * b / a) / a
    to_v = step * b / a + beta
    to_g = -step
    bottom = to_v * to_v * (a + b) + 2.0 * to_v * to_g * (b + c) + to_g * to_g * (c + e)
    second = beta * a / bottom
    weight_v = step + second * to_v
    weight_g = second * to_g

    shape = (wide, lanes)
    lane = lanes_of(shape)
    row = rows_of(shape)
    at_y = base_y + jnp.where(row < rows + FACE, row, row - wide)
    inside_y = (at_y >= 0) & (at_y < total_y)
    place = lax.rem(lane, SW)
    at_strip = base_z + jnp.where(place < 8, place - 8, lanes - 8 + place)
    inside_strip = inside_y & (at_strip >= 0) & (at_strip < total_z)
    small = rows_of((8, lanes))

    def folded(value):
        tail = jnp.where(small < HALO, value[rows : rows + 8], value[rows + 8 :])
        return value[:rows], tail

    def moduli_of(v, g):
        value = weight_v * v + weight_g * g
        return MIN_MODULUS + (1.0 - MIN_MODULUS) * value * value * jnp.abs(value)

    def inverted(total, open_nodes):
        return jnp.where(total > 0.0, open_nodes / jnp.where(total > 0.0, diagonal * total, 1.0), 0.0)

    tall_lane = lanes_of((tall, lanes))
    for source, strip, at in ((node_own, strip_own, mine), (node_other, strip_other, planes - mine)):
        for f in range(4):
            for p in range(planes):
                q = (f % 2) * planes + p
                begin = (2 + f // 2) * tall
                tail = 4 * tall + FACE * (f * planes + p)
                for value, r, n in ((source[f * planes + p], 0, rows), (strip[tail : tail + FACE], rows, FACE)):
                    before = turned(strip[begin + r : begin + r + n], lanes - HALO - (SW * q + 8), 1)
                    value = jnp.where(lanes_of((n, lanes)) < lanes - HALO, value, before)
                    if f == 0:
                        free[at + p, r : r + n] = value
                    else:
                        basis_0[f - 1, at + p, r : r + n] = value
    half = lanes // 2
    left = tall_lane < half
    for pair in range(2):
        at = pair * tall
        lower = either(gx, strip_own[at : at + tall], strip_other[at : at + tall])
        upper = either(gx, strip_other[at : at + tall], strip_own[at : at + tall])
        one = jnp.where(left, lower, turned(upper, half, 1))
        two = jnp.where(left, turned(lower, half, 1), upper)
        for k, value in ((2 * pair, one), (2 * pair + 1, two)):
            if k == 0:
                s_free[...] = value
            else:
                s_basis[0, k - 1] = value

    side = jnp.where(inside_strip, moduli_of(strip_v[...], strip_g[...]), 0.0)
    s_mod = turned(side, 4, 1)
    s_back = jnp.zeros(shape, jnp.float32)
    previous = jnp.zeros(shape, jnp.float32)
    for p in range(count):
        mod = jnp.where(inside_y, moduli_of(window[p], first[p]), 0.0)
        before = turned(side, lanes - HALO - (SW * p + 4), 1)
        across = jnp.where(lane >= lanes - HALO, before, mod)
        head, tail = folded(across)
        modulus[p, :rows] = head
        modulus[p, rows:] = tail
        across = across + turned(jnp.where(lane >= lanes - HALO - 1, before, mod), 1, 1)
        across = across + turned(across, 1, 0)
        head, tail = folded(across + previous)
        previous = across
        inverse[p, :rows] = inverted(head, free[p, :rows])
        inverse[p, rows:] = inverted(tail, free[p, rows:])
        inside = (lane // SW == p) & (place < 12)
        moved = turned(mod, SW * p + 12, 1)
        s_mod = jnp.where(inside, moved, s_mod)
        s_back = jnp.where(lane == (SW * p - 1) % lanes, moved, s_back)
    for p in range(planes):
        filtered[p] = (weight_v * window[mine + p] + weight_g * first[mine + p])[:rows]
    head, tail = folded(s_mod)
    s_modulus[:rows] = head
    s_modulus[rows:] = tail
    across = s_mod + turned(jnp.where(place == SW - 1, s_back, s_mod), 1, 1)
    across = across + turned(across, 1, 0)
    across = across + jnp.where(lane < SW, 0.0, turned(across, SW, 1))
    head, tail = folded(across)
    s_inverse[:rows] = inverted(head, s_free[:rows])
    s_inverse[rows:] = inverted(tail, s_free[rows:])

    lane = lanes_of((8, lanes))
    last_plane = lane >= lanes - SW
    first_plane = lane < SW
    starts = range(0, tall, 8)

    def strip_pairs():
        for c in range(3):
            for r in starts:
                value = s_disp[c, r : r + 8]
                ahead = turned(value, -1, 1)
                s_part[2 * c, r : r + 8] = value + ahead
                s_part[2 * c + 1, r : r + 8] = ahead - value
        for k in range(6):
            for r in starts:
                value = s_part[k, r : r + 8]
                beside = jnp.where(last_plane, 0.0, turned(value, -SW, 1))
                s_pairs[2 * k, r : r + 8] = value + beside
                s_pairs[2 * k + 1, r : r + 8] = beside - value
            for n in (2 * k, 2 * k + 1):
                s_pairs[n, tall : tall + 1] = s_pairs[n, 0:1]

    for c in range(3):
        s_disp[c] = s_inverse[...] * s_basis[0, c]
    strip_pairs()
    for j in range(4):
        for r in starts:
            u = []
            for c in range(3):
                modes = {}
                for g in range(2):
                    for alpha in range(2):
                        k = 2 * (2 * c + g) + alpha
                        now = s_pairs[k, r : r + 8]
                        after = s_pairs[k, r + 1 : r + 9]
                        if (alpha, g) != (0, 0):
                            modes[alpha, 0, g] = now + after
                        modes[alpha, 1, g] = after - now
                u.append(modes)
            f = element_forces(u, s_modulus[r : r + 8])
            for c in range(3):
                for g in range(2):
                    for alpha in range(2):
                        k = 2 * (2 * c + g) + alpha
                        diff = f[c][alpha, 1, g]
                        if (alpha, g) == (0, 0):
                            s_near[k, r : r + 8] = -diff
                            s_far[k, r + 8 : r + 16] = diff
                        else:
                            total = f[c][alpha, 0, g]
                            s_near[k, r : r + 8] = total - diff
                            s_far[k, r + 8 : r + 16] = total + diff
        for k in range(12):
            s_far[k, 7:8] = s_far[k, tall + 7 : tall + 8]
        for k in range(6):
            for r in starts:
                total = s_near[2 * k, r : r + 8] + s_far[2 * k, r + 7 : r + 15]
                diff = s_near[2 * k + 1, r : r + 8] + s_far[2 * k + 1, r + 7 : r + 15]
                upper = jnp.where(first_plane, 0.0, turned(total + diff, SW, 1))
                s_part[k, r : r + 8] = (total - diff) + upper
        for c in range(3):
            for r in starts:
                total = s_part[2 * c, r : r + 8]
                diff = s_part[2 * c + 1, r : r + 8]
                out = (total - diff) + turned(total + diff, 1, 1)
                new = s_free[r : r + 8] * out - SHIFTS[j] * s_basis[j, c, r : r + 8]
                s_basis[j + 1, c, r : r + 8] = new
                if j < 3:
                    s_disp[c, r : r + 8] = s_inverse[r : r + 8] * new
        if j < 3:
            strip_pairs()

    def spread_z(c, p, r, disp):
        ahead = turned(disp, -1, 1)
        pairs[2 * c, p, r : r + 8] = disp + ahead
        pairs[2 * c + 1, p, r : r + 8] = ahead - disp

    def close_rows(p):
        for k in range(6):
            pairs[k, p, tall : tall + 1] = pairs[k, p, 0:1]

    for k in range(6):
        pairs[k, count] = jnp.zeros(pairs.shape[2:], jnp.float32)

    def start_plane(p, carry):
        for r in starts:
            for c in range(3):
                spread_z(c, p, r, inverse[p, r : r + 8] * basis_0[c, p, r : r + 8])
        close_rows(p)
        return carry

    lax.fori_loop(0, count, start_plane, 0)

    def along_rows(p, r):
        result = []
        for k in range(6):
            now = pairs[k, p, r : r + 8]
            after = pairs[k, p, r + 1 : r + 9]
            result.append((now + after, after - now))
        return result

    for j in range(4):
        low = gx * j
        high = count - 1 - j + gx * (j + 1)
        for r in starts:
            for k, both in enumerate(along_rows(low, r)):
                for beta_ in range(2):
                    kept[2 * k + beta_, r : r + 8] = both[beta_]
                    carried[2 * k + beta_, r : r + 8] = jnp.zeros((8, lanes), jnp.float32)

        def layer(p, state, j=j, low=low):
            for r in starts:
                upper_rows = along_rows(p + 1, r)
                u = []
                for c in range(3):
                    modes = {}
                    for g in range(2):
                        for beta_ in range(2):
                            k = 2 * (2 * c + g) + beta_
                            now = kept[k, r : r + 8]
                            above = upper_rows[2 * c + g][beta_]
                            if (beta_, g) != (0, 0):
                                modes[0, beta_, g] = now + above
                            modes[1, beta_, g] = above - now
                            kept[k, r : r + 8] = above
                    u.append(modes)
                f = element_forces(u, modulus[p, r : r + 8])
                for c in range(3):
                    for g in range(2):
                        t_beta = []
                        for beta_ in range(2):
                            k = 2 * (2 * c + g) + beta_
                            diff = f[c][1, beta_, g]
                            before = carried[k, r : r + 8]
                            if (beta_, g) == (0, 0):
                                t_beta.append(before - diff)
                                carried[k, r : r + 8] = diff
                            else:
                                total = f[c][0, beta_, g]
                                t_beta.append(before + (total - diff))
                                carried[k, r : r + 8] = total + diff
                        near[2 * c + g, r : r + 8] = t_beta[0] - t_beta[1]
                        far[2 * c + g, r + 8 : r + 16] = t_beta[0] + t_beta[1]
            for k in range(6):
                far[k, 7:8] = far[k, tall + 7 : tall + 8]
            @pl.when((p > low) | (gx == 0))
            def finish():
                fresh = {}
                for r in starts:
                    open_nodes = free[p, r : r + 8]
                    for c in range(3):
                        total = near[2 * c, r : r + 8] + far[2 * c, r + 7 : r + 15]
                        diff = near[2 * c + 1, r : r + 8] + far[2 * c + 1, r + 7 : r + 15]
                        out = (total - diff) + turned(total + diff, 1, 1)
                        fresh[r, c] = open_nodes * out - SHIFTS[j] * basis[j][c, p, r : r + 8]
                for r in starts:
                    for c in range(3):
                        basis[j + 1][c, p, r : r + 8] = fresh[r, c]
                        if j < 3:
                            fresh[r, c] = inverse[p, r : r + 8] * fresh[r, c]
                if j < 3:
                    ahead = {key: turned(value, -1, 1) for key, value in fresh.items()}
                    for (r, c), value in fresh.items():
                        pairs[2 * c, p, r : r + 8] = value + ahead[r, c]
                        pairs[2 * c + 1, p, r : r + 8] = ahead[r, c] - value
                if j < 3:
                    close_rows(p)

            return state

        lax.fori_loop(low, high, layer, 0)

    order = [(i, k) for i in range(4) for k in range(i, 5)]
    zero = jnp.zeros((8, lanes), jnp.float32)

    def add_dots(p, sums):
        plane = mine + p
        sums = list(sums)
        for r in range(0, rows, 8):
            inv = inverse[plane, r : r + 8]
            scale[p, r : r + 8] = inv
            for c in range(3):
                ys = [basis[i][c, plane, r : r + 8] for i in range(5)]
                ws = [inv * y for y in ys[:4]]
                for i in range(5):
                    fields[i, c, p, r : r + 8] = ys[i]
                for n, (i, k) in enumerate(order):
                    sums[n] = sums[n] + ws[i] * ys[k]
        return tuple(sums)

    main = lax.fori_loop(0, planes, add_dots, (zero,) * len(order))
    extra = [zero] * len(order)
    for r in range(0, rows, 8):
        inv = s_inverse[r : r + 8]
        strip_scale[r : r + 8] = inv
        for c in range(3):
            ys = [s_basis[i, c, r : r + 8] for i in range(5)]
            ws = [inv * y for y in ys[:4]]
            for i in range(5):
                strip_fields[i, c, r : r + 8] = ys[i]
            for n, (i, k) in enumerate(order):
                extra[n] = extra[n] + ws[i] * ys[k]
    place = lax.rem(lane, SW)
    own_lanes = (place >= 4) & (place < 12) & (lane // (SW * planes) == gx)
    sums = [
        jnp.where(lane < lanes - 8, value, 0.0) + jnp.where(own_lanes, more, 0.0) for value, more in zip(main, extra)
    ]
    spread(sums, dots)


def combine_kernel(dots, basis, strips, scale, strip_scale, displacement, residual, ends):
    order = [(i, k) for i in range(4) for k in range(i, 5)]
    gram = {}
    for value, (i, k) in zip(gathered(dots, len(order)), order):
        gram[i, k] = gram[k, i] = value
    zero = jnp.zeros((1, 1), jnp.float32)
    one = jnp.ones((1, 1), jnp.float32)
    res = [one]
    search = [one]
    disp = []
    res_dot = gram[0, 0]
    for iteration in range(4):
        image = [zero] * (iteration + 2)
        for i, value in enumerate(search):
            image[i] = image[i] + SHIFTS[i] * value
            image[i + 1] = image[i + 1] + value
        curve = zero
        for i, left in enumerate(search):
            inner = zero
            for k, right in enumerate(image):
                inner = inner + gram[i, k] * right
            curve = curve + left * inner
        step = res_dot / curve
        disp = [d + step * s for d, s in zip(disp + [zero], search)]
        res = [r - step * q for r, q in zip(res + [zero], image)]
        if iteration < 3:
            new_dot = zero
            for i, left in enumerate(res):
                inner = zero
                for k, right in enumerate(res):
                    inner = inner + gram[i, k] * right
                new_dot = new_dot + left * inner
            search = [r + new_dot / res_dot * s for r, s in zip(res, search + [zero])]
            res_dot = new_dot
    planes, rows, lanes = scale.shape
    disp = [jnp.broadcast_to(d, (8, lanes)) for d in disp]
    res = [jnp.broadcast_to(r, (8, lanes)) for r in res]

    def combined(ys, inv):
        first = disp[0] * ys[0]
        second = res[0] * ys[0]
        for i in range(1, 5):
            second = second + res[i] * ys[i]
            if i < 4:
                first = first + disp[i] * ys[i]
        return inv * first, second

    gx = lax.axis_index("gx")
    for r in range(0, rows, 8):
        for c in range(3):
            both = combined([strips[i, c, r : r + 8] for i in range(5)], strip_scale[r : r + 8])
            for n, value in enumerate(both):
                ends[3 * n + c, r : r + 8] = either(gx, value, turned(value, lanes // 2, 1))
    lane = lanes_of((8, lanes))
    for p in range(planes):
        for r in range(0, rows, 8):
            inv = scale[p, r : r + 8]
            for c in range(3):
                both = combined([basis[i, c, p, r : r + 8] for i in range(5)], inv)
                for n, out in enumerate((displacement, residual)):
                    end = turned(ends[3 * n + c, r : r + 8], lanes - 8 - (SW * p + 4), 1)
                    out[c, p, r : r + 8] = jnp.where(lane < lanes - 8, both[n], end)


def call(kernel, outs, *args, scratch=()):
    return pl.pallas_call(
        kernel,
        out_shape=tuple(jax.ShapeDtypeStruct(shape, jnp.float32) for shape in outs),
        in_specs=[pl.BlockSpec(memory_space=pltpu.VMEM)] * len(args),
        out_specs=tuple(pl.BlockSpec(memory_space=pltpu.VMEM) for _ in outs),
        scratch_shapes=list(scratch),
        compiler_params=pltpu.CompilerParams(vmem_limit_bytes=VMEM_LIMIT),
    )(*args)


def swapped(value, axis, first):
    count = lax.axis_size(axis)
    pairs = [(i, i + 1) for i in range(first, count - 1, 2)]
    if not pairs:
        return jnp.zeros_like(value)
    return lax.ppermute(value, axis, pairs + [(j, i) for i, j in pairs])


def paired_shards(density, fixed_mask, load_mask, load_values):
    planes, rows, lanes = density.shape
    devices = 1
    for axis in AXES:
        devices *= lax.axis_size(axis)
    grid = (rows * lax.axis_size("gy"), lanes * lax.axis_size("gz"))
    count = 2 * planes
    wide, tall = rows + 2 * FACE, rows + FACE
    face = (4 * planes, FACE, lanes)
    row = (devices, 1, lanes)
    f32 = jnp.float32
    density_other = swapped(density, "gx", 0)
    density_own, nodes = call(
        node_kernel, (density.shape, (4 * planes, rows, lanes)), density, fixed_mask, load_mask, load_values
    )
    nodes_other = swapped(nodes, "gx", 0)
    send_a, send_b = call(face_kernel, (face, face), density_own, density_other, nodes)
    window, tails, strips = call(
        strip_kernel,
        ((count, wide, lanes), (4 * planes, FACE, lanes), (wide + 2 * tall, lanes)),
        density_own, density_other, nodes, swapped(send_a, "gy", 0), swapped(send_b, "gy", 1),
    )
    from_a, from_b = swapped(strips, "gz", 0), swapped(strips, "gz", 1)
    first, strip_v, strip_g, node_strips, dots = call(
        functools.partial(filter_kernel, grid),
        ((count, wide, lanes), (wide, lanes), (wide, lanes), (4 * tall + 4 * planes * FACE, lanes), row),
        window, tails, strips, from_a, from_b,
    )
    strips_other = swapped(node_strips, "gx", 0)
    dots = lax.all_to_all(dots, AXES, 0, 0, tiled=True)
    diagonal = float(element_table()[0, 0, 0, 0])
    plane, taller = (tall, lanes), (tall + 8, lanes)
    many = (count,) + plane
    filtered, basis, strip_basis, scale, strip_scale, dots = call(
        functools.partial(solve_kernel, grid, diagonal),
        ((planes, rows, lanes), (5, 3, planes, rows, lanes), (5, 3, rows, lanes), (planes, rows, lanes), (rows, lanes), row),
        window, first, strip_v, strip_g, dots, nodes, nodes_other, node_strips, strips_other,
        scratch=[
            pltpu.VMEM(shape, f32)
            for shape in (
                *(((3,) + many,) * 5), many, many, many, (6, count + 1) + taller, (12,) + plane, (12,) + plane, (6,) + plane, (6,) + taller,
                (5, 3) + plane, plane, plane, plane, (12,) + taller, (12,) + plane, (12,) + taller, (6,) + plane, (3,) + plane,
            )
        ],
    )
    dots = lax.all_to_all(dots, AXES, 0, 0, tiled=True)
    displacement, residual = call(
        combine_kernel, (load_values.shape, load_values.shape), dots, basis, strip_basis, scale, strip_scale,
        scratch=[pltpu.VMEM((6, rows, lanes), f32)],
    )
    return (filtered, displacement, residual)


def shards(density, fixed_mask, load_mask, load_values):
    planes, rows, lanes = density.shape
    if lax.axis_size("gx") == 2 and 2 * planes * SW == lanes and lanes == 128 and rows % 8 == 0:
        return paired_shards(density, fixed_mask, load_mask, load_values)
    return general_shards(density, fixed_mask, load_mask, load_values)


def solution(mesh):
    return jax.shard_map(
        shards,
        mesh=mesh,
        in_specs=(
            P("gx", "gy", "gz"),
            P("gx", "gy", "gz"),
            P("gx", "gy", "gz"),
            P(None, "gx", "gy", "gz"),
        ),
        out_specs=(P("gx", "gy", "gz"), P(None, "gx", "gy", "gz"), P(None, "gx", "gy", "gz")),
        check_vma=False,
    )
```

```python
import functools

import jax
import jax.numpy as jnp
import numpy as np
from jax import lax
from jax.experimental import pallas as pl
from jax.experimental.pallas import tpu as pltpu
from jax.sharding import PartitionSpec as P

FILTER_ITERS = 2
SOLVE_ITERS = 4


MIN_MODULUS = 0.001
filter_weight = 0.75


def passed_along(value, axis, steps):
    count = lax.axis_size(axis)
    initial, last = (max(0, -steps), min(count, count - steps))
    return lax.ppermute(value, axis, [(source, source + steps) for source in range(initial, last)])


def padded_2(block, sides, width):
    for axis, dim in sides:
        count = lax.axis_size(axis)
        forward = [(i, i + 1) for i in range(count - 1)]
        backward = [(target, source) for source, target in forward]
        low = lax.ppermute(
            lax.slice_in_dim(block, block.shape[dim] - width, None, axis=dim), axis, forward
        )
        high = lax.ppermute(lax.slice_in_dim(block, 0, width, axis=dim), axis, backward)
        block = jnp.concatenate([low, block, high], axis=dim)
    return block


def element_table():
    poisson = 0.3
    lame_first = poisson / ((1.0 + poisson) * (1.0 - 2.0 * poisson))
    lame_shear = 1.0 / (2.0 * (1.0 + poisson))
    elastic = np.zeros((6, 6))
    elastic[:3, :3] = lame_first
    for index in range(3):
        elastic[index, index] += 2.0 * lame_shear
        elastic[index + 3, index + 3] = lame_shear
    gauss_value = 1.0 / np.sqrt(3.0)
    matrix = np.zeros((24, 24))
    for first in (-gauss_value, gauss_value):
        for second in (-gauss_value, gauss_value):
            for third in (-gauss_value, gauss_value):
                gauss_point = (first, second, third)
                strain = np.zeros((6, 24))
                for corner in range(8):
                    corner_signs = [
                        2 * (corner >> 2 & 1) - 1,
                        2 * (corner >> 1 & 1) - 1,
                        2 * (corner & 1) - 1,
                    ]
                    factors = [1.0 + corner_signs[d] * gauss_point[d] for d in range(3)]
                    slopes = [
                        corner_signs[d] * factors[(d + 1) % 3] * factors[(d + 2) % 3] / 4.0
                        for d in range(3)
                    ]
                    column = 3 * corner
                    strain[0, column] = slopes[0]
                    strain[1, column + 1] = slopes[1]
                    strain[2, column + 2] = slopes[2]
                    strain[3, column] = slopes[1]
                    strain[3, column + 1] = slopes[0]
                    strain[4, column + 1] = slopes[2]
                    strain[4, column + 2] = slopes[1]
                    strain[5, column] = slopes[2]
                    strain[5, column + 2] = slopes[0]
                matrix += strain.T @ elastic @ strain / 8.0
    return matrix.reshape(8, 3, 8, 3).transpose(0, 2, 1, 3)


def corner_offsets(corner):
    return (corner >> 2 & 1, corner >> 1 & 1, corner & 1)


def apply_stiffness(disp_pad, mod_pad, extent):
    stiffness = jnp.asarray(element_table(), jnp.float32)
    size_x, size_y, size_z = extent
    result = jnp.zeros((3, size_x, size_y, size_z), jnp.float32)
    for corner_a in range(8):
        offs_a = corner_offsets(corner_a)
        moduli_part = mod_pad[
            1 - offs_a[0] : 1 - offs_a[0] + size_x,
            1 - offs_a[1] : 1 - offs_a[1] + size_y,
            1 - offs_a[2] : 1 - offs_a[2] + size_z,
        ]
        inner_sum = jnp.zeros((3, size_x, size_y, size_z), jnp.float32)
        for corner_b in range(8):
            offs_b = corner_offsets(corner_b)
            start_x = 1 - offs_a[0] + offs_b[0]
            start_y = 1 - offs_a[1] + offs_b[1]
            start_z = 1 - offs_a[2] + offs_b[2]
            shifted = disp_pad[
                :,
                start_x : start_x + size_x,
                start_y : start_y + size_y,
                start_z : start_z + size_z,
            ]
            for comp in range(3):
                inner_sum = (
                    inner_sum
                    + stiffness[corner_a, corner_b, :, comp][:, None, None, None]
                    * shifted[comp][None]
                )
        result = result + moduli_part[None] * inner_sum
    return result


def jacobi_diagonal(mod_pad, extent):
    stiffness = jnp.asarray(element_table(), jnp.float32)
    size_x, size_y, size_z = extent
    diagonal = jnp.zeros((3, size_x, size_y, size_z), jnp.float32)
    for corner_a in range(8):
        offs_a = corner_offsets(corner_a)
        moduli_part = mod_pad[
            1 - offs_a[0] : 1 - offs_a[0] + size_x,
            1 - offs_a[1] : 1 - offs_a[1] + size_y,
            1 - offs_a[2] : 1 - offs_a[2] + size_z,
        ]
        block_diag = jnp.stack([stiffness[corner_a, corner_a, comp, comp] for comp in range(3)])
        diagonal = diagonal + moduli_part[None] * block_diag[:, None, None, None]
    return diagonal


def face_sum(padded):
    beside = padded[2:, 1:-1, 1:-1] + padded[:-2, 1:-1, 1:-1]
    beside = beside + padded[1:-1, 2:, 1:-1] + padded[1:-1, :-2, 1:-1]
    return beside + padded[1:-1, 1:-1, 2:] + padded[1:-1, 1:-1, :-2]


def edge_count(global_index, total):
    return (global_index > 0).astype(jnp.float32) + (global_index < total - 1).astype(jnp.float32)


def neighbour_counts(extent):
    size_x, size_y, size_z = extent
    index_x = lax.axis_index("gx") * size_x + jnp.arange(size_x, dtype=jnp.int32)
    index_y = lax.axis_index("gy") * size_y + jnp.arange(size_y, dtype=jnp.int32)
    index_z = lax.axis_index("gz") * size_z + jnp.arange(size_z, dtype=jnp.int32)
    count_x = edge_count(index_x, size_x * lax.axis_size("gx"))
    count_y = edge_count(index_y, size_y * lax.axis_size("gy"))
    count_z = edge_count(index_z, size_z * lax.axis_size("gz"))
    return count_x[:, None, None] + count_y[None, :, None] + count_z[None, None, :]


def lower_moduli(moduli):
    rim_x = passed_along(moduli[-1:], "gx", 1)
    extended = jnp.concatenate([rim_x, moduli], axis=0)
    rim_y = passed_along(extended[:, -1:], "gy", 1)
    extended = jnp.concatenate([rim_y, extended], axis=1)
    rim_z = passed_along(extended[:, :, -1:], "gz", 1)
    return jnp.concatenate([rim_z, extended], axis=2)


def displacement_halo(field):
    return padded_2(field, (("gx", 1), ("gy", 2), ("gz", 3)), 1)


def residual_dot(first, second):
    return lax.psum(jnp.sum(first * second), ("gx", "gy", "gz"))


def curvature_dot(first, second):
    return lax.psum(jnp.sum(first * second), ("gx", "gy", "gz"))


def conjugate(operator, precond, force, iters):
    iterate = jnp.zeros_like(force)
    residual = force
    search = precond(residual)
    direction = search
    res_dot = residual_dot(residual, search)
    for iteration in range(iters):
        image = operator(direction)
        step_size = res_dot / curvature_dot(direction, image)
        iterate = iterate + step_size * direction
        residual = residual - step_size * image
        if iteration + 1 < iters:
            search = precond(residual)
            new_dot = residual_dot(residual, search)
            direction = search + new_dot / res_dot * direction
            res_dot = new_dot
    return (iterate, residual)


def general_shards(density, fixed_mask, load_mask, load_values):
    extent = density.shape
    counts = neighbour_counts(extent)

    def filter_apply(field):
        padded = padded_2(field, (("gx", 0), ("gy", 1), ("gz", 2)), 1)
        return field + filter_weight * (counts * field - face_sum(padded))

    def identity(field):
        return field

    filtered, unused = conjugate(filter_apply, identity, density, FILTER_ITERS)
    moduli = MIN_MODULUS + (1.0 - MIN_MODULUS) * filtered * filtered * jnp.abs(filtered)
    mod_pad = lower_moduli(moduli)
    free_nodes = (1 - fixed_mask).astype(jnp.float32)
    force = free_nodes[None] * load_mask.astype(jnp.float32)[None] * load_values
    inverse_diag = free_nodes[None] / jacobi_diagonal(mod_pad, extent)

    def elastic_apply(field):
        return free_nodes[None] * apply_stiffness(displacement_halo(field), mod_pad, extent)

    def jacobi(field):
        return inverse_diag * field

    displacement, residual = conjugate(elastic_apply, jacobi, force, SOLVE_ITERS)
    return (filtered, displacement, residual)


HALO = 4
SW = 16
FACE = 8
AXES = ("gx", "gy", "gz")
SHIFTS = (1.2, 0.4, 2.0, 0.8)
VMEM_LIMIT = 24 * 1024 * 1024
POISSON = 0.3
LAME = POISSON / ((1.0 + POISSON) * (1.0 - 2.0 * POISSON))
SHEAR = 1.0 / (2.0 * (1.0 + POISSON))
AXIAL = LAME + 2.0 * SHEAR
MODES = [(a, b, g) for a in range(2) for b in range(2) for g in range(2)]


def lanes_of(shape):
    return lax.broadcasted_iota(jnp.int32, shape, len(shape) - 1)


def rows_of(shape):
    return lax.broadcasted_iota(jnp.int32, shape, len(shape) - 2)


def turned(value, shift, axis):
    size = value.shape[axis]
    if isinstance(shift, int):
        shift = shift % size
        if shift == 0:
            return value
    else:
        shift = lax.rem(shift + 4 * size, size)
    return pltpu.roll(value, shift, axis)


def either(flag, first, second):
    return jnp.where(jnp.full(first.shape, flag, jnp.int32) == 0, first, second)


def node_kernel(density, fixed, load_mask, load_values, held, nodes):
    planes = density.shape[0]
    held[...] = density[...]
    for p in range(planes):
        free = (1 - fixed[p]).astype(jnp.float32)
        loaded = free * load_mask[p].astype(jnp.float32)
        nodes[p] = free
        for c in range(3):
            nodes[(1 + c) * planes + p] = loaded * load_values[c, p]


def face_kernel(density, other, nodes, send_a, send_b):
    planes, rows, lanes = density.shape
    half = 2 * planes
    gx = lax.axis_index("gx")
    odd = lax.rem(lax.axis_index("gy"), 2)
    top = rows - FACE
    row = rows_of((FACE, lanes))
    for p in range(planes):
        for source, at in ((density, gx * planes), (other, planes - gx * planes)):
            low, high = source[p, :FACE], source[p, top:]
            send_a[at + p] = either(odd, high, low)
            send_b[at + p] = either(odd, low, high)
    for q in range(half):
        low = jnp.where(row < HALO, nodes[q, :FACE], turned(nodes[q + half, :FACE], HALO, 0))
        high = jnp.where(row < HALO, turned(nodes[q + half, top:], HALO, 0), nodes[q, top:])
        send_a[half + q] = either(odd, high, low)
        send_b[half + q] = either(odd, low, high)


def strip_kernel(density, other, nodes, from_a, from_b, window, tails, strips):
    planes, rows, lanes = density.shape
    wide, tall = rows + 2 * FACE, rows + FACE
    half = 2 * planes
    mine = lax.axis_index("gx") * planes
    odd_y = lax.rem(lax.axis_index("gy"), 2)
    row = rows_of((FACE, lanes))
    for source, at in ((density, mine), (other, planes - mine)):
        for p in range(planes):
            window[at + p, :rows] = source[p]
    for p in range(half):
        window[p, rows : rows + FACE] = either(odd_y, from_a[p], from_b[p])
        window[p, rows + FACE :] = either(odd_y, from_b[p], from_a[p])
        above = either(odd_y, from_a[half + p], from_b[half + p])
        below = either(odd_y, from_b[half + p], from_a[half + p])
        tails[p] = jnp.where(row < HALO, above, below)
        tails[half + p] = jnp.where(row < HALO, turned(above, HALO, 0), turned(below, HALO, 0))
    for begin, end in ((0, rows), (rows, wide)):
        lane = lanes_of((end - begin, lanes))
        packed = jnp.zeros((end - begin, lanes), jnp.float32)
        for p in range(half):
            packed = jnp.where(lane // SW == p, turned(window[p, begin:end], SW * p + 8, 1), packed)
        strips[begin:end] = packed
    for pair in range(2):
        at = wide + pair * tall
        for source, size, begin in ((nodes, rows, at), (tails, FACE, at + rows)):
            lane = lanes_of((size, lanes))
            packed = jnp.zeros((size, lanes), jnp.float32)
            for q in range(half):
                packed = jnp.where(lane // SW == q, turned(source[half * pair + q], SW * q + 12, 1), packed)
            strips[begin : begin + size] = packed


def filter_kernel(grid, window, tails, strips, from_a, from_b, first, strip_v, strip_g, node_strips, dots):
    count, wide, lanes = window.shape
    rows = wide - 2 * FACE
    planes = count // 2
    total_y, total_z = grid
    mine = lax.axis_index("gx") * planes
    odd_z = lax.rem(lax.axis_index("gz"), 2)
    base_y = lax.axis_index("gy") * rows
    base_z = lax.axis_index("gz") * lanes
    shape = (wide, lanes)
    lane = lanes_of(shape)
    row = rows_of(shape)
    place = lax.rem(lane, SW)
    strip_v[...] = jnp.where(
        place < 8, either(odd_z, from_b[:wide], from_a[:wide]), either(odd_z, from_a[:wide], from_b[:wide])
    )
    at_y = base_y + jnp.where(row < rows + FACE, row, row - wide)
    pass_y = ((at_y >= 0) & (at_y < total_y - 1)).astype(jnp.float32)
    pass_z = (base_z + lane < total_z - 1).astype(jnp.float32)
    back_z = (base_z + lane > 0).astype(jnp.float32)
    at_strip = base_z + jnp.where(place < 8, place - 8, lanes - 8 + place)
    strip_pass = ((at_strip >= 0) & (at_strip < total_z - 1)).astype(jnp.float32)
    strip_back = ((at_strip >= 1) & (at_strip < total_z)).astype(jnp.float32)

    def along_y(value):
        ahead = (turned(value, -1, 0) - value) * pass_y
        return turned(ahead, 1, 0) - ahead

    def laplace(source, side, q, p, lower, upper):
        value = source[p]
        result = (value - source[upper]) + (value - source[lower])
        result = result + along_y(value)
        ahead = jnp.where(lane == lanes - 1, turned(side, lanes - 1 - (SW * q + 8), 1), turned(value, -1, 1))
        behind = jnp.where(lane == 0, turned(side, 0 - (SW * q + 7), 1), turned(value, 1, 1))
        result = result + (value - ahead) * pass_z + (value - behind) * back_z
        return filter_weight * result

    value = strip_v[...]
    for p in range(count):
        first[p] = laplace(window, value, p, p, max(p - 1, 0), min(p + 1, count - 1))
    edge_low = jnp.zeros(shape, jnp.float32)
    edge_high = edge_low
    for p in range(count):
        edge_low = jnp.where(lane == SW * p + 7, turned(window[p], SW * p + 7, 1), edge_low)
        edge_high = jnp.where(lane == SW * p + 8, turned(window[p], SW * p + 8 - (lanes - 1), 1), edge_high)
    ahead = jnp.where(place == 7, edge_low, turned(value, -1, 1))
    behind = jnp.where(place == 8, edge_high, turned(value, 1, 1))
    result = along_y(value) + (value - ahead) * strip_pass + (value - behind) * strip_back
    ahead = jnp.where(lane < lanes - SW, turned(value, -SW, 1) - value, 0.0)
    result = result + turned(ahead, SW, 1) - ahead
    strip_g[...] = filter_weight * result

    value = strip_g[...]
    value = either(mine, value, turned(value, lanes // 2, 1))
    sums = [jnp.zeros((8, lanes), jnp.float32)] * 4
    for p in range(planes):
        plane = mine + p
        w = window[plane][:rows]
        g = first[plane][:rows]
        gg = laplace(first, value, p, plane, jnp.maximum(plane - 1, 0), jnp.minimum(plane + 1, count - 1))[:rows]
        terms = (w * w, w * g, g * g, g * gg)
        sums = [s + jnp.sum(t.reshape(rows // 8, 8, lanes), axis=0) for s, t in zip(sums, terms)]
    spread(sums, dots)
    half = strips.shape[0] - wide
    place = lax.rem(lanes_of((half, lanes)), SW)
    node_strips[:half] = jnp.where(place < 12, strips[wide:], either(odd_z, from_a[wide:], from_b[wide:]))
    node_strips[half : 2 * half] = either(odd_z, from_b[wide:], from_a[wide:])
    for q in range(tails.shape[0]):
        node_strips[2 * half + FACE * q : 2 * half + FACE * (q + 1)] = tails[q]


def spread(sums, dots):
    lanes = dots.shape[-1]
    lane = lanes_of((1, lanes))
    line = jnp.zeros((1, lanes), jnp.float32)
    for k, value in enumerate(sums):
        value = jnp.sum(jnp.sum(value, axis=0, keepdims=True), axis=1, keepdims=True)
        line = jnp.where(lane == k, value, line)
    for k in range(dots.shape[0]):
        dots[k] = line


def gathered(dots, count):
    line = jnp.sum(dots[...], axis=0)
    lane = lanes_of(line.shape)
    return [
        jnp.sum(jnp.where(lane == k, line, 0.0), axis=1, keepdims=True) for k in range(count)
    ]


def element_forces(u, modulus):
    shear = modulus * (SHEAR / 16.0)
    shear_3 = modulus * (SHEAR / 48.0)
    twist = modulus * ((AXIAL + 2.0 * SHEAR) / 144.0)
    normal = modulus * (2.0 * SHEAR / 16.0)
    paired = modulus * ((AXIAL + SHEAR) / 48.0)
    x, y, z = u
    f = [{}, {}, {}]
    trace = (x[1, 0, 0] + y[0, 1, 0] + z[0, 0, 1]) * (LAME / (2.0 * SHEAR))
    f[0][1, 0, 0] = (trace + x[1, 0, 0]) * normal
    f[1][0, 1, 0] = (trace + y[0, 1, 0]) * normal
    f[2][0, 0, 1] = (trace + z[0, 0, 1]) * normal
    ratio = LAME / (AXIAL + SHEAR)
    for (c, m), (d, n) in (
        ((0, (1, 1, 0)), (2, (0, 1, 1))),
        ((1, (1, 1, 0)), (2, (1, 0, 1))),
        ((0, (1, 0, 1)), (1, (0, 1, 1))),
    ):
        f[c][m] = (u[c][m] + ratio * u[d][n]) * paired
        f[d][n] = (u[d][n] + ratio * u[c][m]) * paired
    for (c, m), (d, n) in (
        ((0, (0, 1, 0)), (1, (1, 0, 0))),
        ((1, (0, 0, 1)), (2, (0, 1, 0))),
        ((0, (0, 0, 1)), (2, (1, 0, 0))),
    ):
        f[c][m] = f[d][n] = (u[c][m] + u[d][n]) * shear
    three = ((0, (0, 1, 1)), (1, (1, 0, 1)), (2, (1, 1, 0)))
    both = x[0, 1, 1] + y[1, 0, 1] + z[1, 1, 0]
    for c, m in three:
        f[c][m] = (both + u[c][m]) * shear_3
    for c in range(3):
        f[c][1, 1, 1] = u[c][1, 1, 1] * twist
    return f


def solve_kernel(
    grid, diagonal, window, first, strip_v, strip_g, filter_dots, node_own, node_other, strip_own, strip_other,
    filtered, fields, strip_fields, scale, strip_scale, dots,
    basis_0, basis_1, basis_2, basis_3, basis_4, modulus, inverse, free, pairs_0, pairs_1, kept, carried, near, far,
    s_basis, s_modulus, s_inverse, s_free, s_pairs, s_near, s_far, s_part, s_disp,
):
    basis = (basis_0, basis_1, basis_2, basis_3, basis_4)
    count, wide, lanes = window.shape
    rows = wide - 2 * FACE
    tall = rows + FACE
    planes = count // 2
    total_y, total_z = grid
    gx = lax.axis_index("gx")
    base_y = lax.axis_index("gy") * rows
    base_z = lax.axis_index("gz") * lanes
    mine = gx * planes

    a, b, c, e = gathered(filter_dots, 4)
    step = a / (a + b)
    beta = step * step * (c - b * b / a) / a
    to_v = step * b / a + beta
    to_g = -step
    bottom = to_v * to_v * (a + b) + 2.0 * to_v * to_g * (b + c) + to_g * to_g * (c + e)
    second = beta * a / bottom
    weight_v = step + second * to_v
    weight_g = second * to_g

    shape = (wide, lanes)
    lane = lanes_of(shape)
    row = rows_of(shape)
    at_y = base_y + jnp.where(row < rows + FACE, row, row - wide)
    inside_y = (at_y >= 0) & (at_y < total_y)
    place = lax.rem(lane, SW)
    at_strip = base_z + jnp.where(place < 8, place - 8, lanes - 8 + place)
    inside_strip = inside_y & (at_strip >= 0) & (at_strip < total_z)
    small = rows_of((8, lanes))

    def folded(value):
        tail = jnp.where(small < HALO, value[rows : rows + 8], value[rows + 8 :])
        return value[:rows], tail

    def moduli_of(v, g):
        value = weight_v * v + weight_g * g
        return MIN_MODULUS + (1.0 - MIN_MODULUS) * value * value * jnp.abs(value)

    def inverted(total, open_nodes):
        return jnp.where(total > 0.0, open_nodes / jnp.where(total > 0.0, diagonal * total, 1.0), 0.0)

    tall_lane = lanes_of((tall, lanes))
    for source, strip, at in ((node_own, strip_own, mine), (node_other, strip_other, planes - mine)):
        for f in range(4):
            for p in range(planes):
                q = (f % 2) * planes + p
                begin = (2 + f // 2) * tall
                tail = 4 * tall + FACE * (f * planes + p)
                for value, r, n in ((source[f * planes + p], 0, rows), (strip[tail : tail + FACE], rows, FACE)):
                    before = turned(strip[begin + r : begin + r + n], lanes - HALO - (SW * q + 8), 1)
                    value = jnp.where(lanes_of((n, lanes)) < lanes - HALO, value, before)
                    if f == 0:
                        free[at + p, r : r + n] = value
                    else:
                        basis_0[f - 1, at + p, r : r + n] = value
    half = lanes // 2
    left = tall_lane < half
    for pair in range(2):
        at = pair * tall
        lower = either(gx, strip_own[at : at + tall], strip_other[at : at + tall])
        upper = either(gx, strip_other[at : at + tall], strip_own[at : at + tall])
        one = jnp.where(left, lower, turned(upper, half, 1))
        two = jnp.where(left, turned(lower, half, 1), upper)
        for k, value in ((2 * pair, one), (2 * pair + 1, two)):
            if k == 0:
                s_free[...] = value
            else:
                s_basis[0, k - 1] = value

    side = jnp.where(inside_strip, moduli_of(strip_v[...], strip_g[...]), 0.0)
    s_mod = turned(side, 4, 1)
    s_back = jnp.zeros(shape, jnp.float32)
    previous = jnp.zeros(shape, jnp.float32)
    for p in range(count):
        mod = jnp.where(inside_y, moduli_of(window[p], first[p]), 0.0)
        before = turned(side, lanes - HALO - (SW * p + 4), 1)
        across = jnp.where(lane >= lanes - HALO, before, mod)
        head, tail = folded(across)
        modulus[p, :rows] = head
        modulus[p, rows:] = tail
        across = across + turned(jnp.where(lane >= lanes - HALO - 1, before, mod), 1, 1)
        across = across + turned(across, 1, 0)
        head, tail = folded(across + previous)
        previous = across
        inverse[p, :rows] = inverted(head, free[p, :rows])
        inverse[p, rows:] = inverted(tail, free[p, rows:])
        inside = (lane // SW == p) & (place < 12)
        moved = turned(mod, SW * p + 12, 1)
        s_mod = jnp.where(inside, moved, s_mod)
        s_back = jnp.where(lane == (SW * p - 1) % lanes, moved, s_back)
    for p in range(planes):
        filtered[p] = (weight_v * window[mine + p] + weight_g * first[mine + p])[:rows]
    head, tail = folded(s_mod)
    s_modulus[:rows] = head
    s_modulus[rows:] = tail
    across = s_mod + turned(jnp.where(place == SW - 1, s_back, s_mod), 1, 1)
    across = across + turned(across, 1, 0)
    across = across + jnp.where(lane < SW, 0.0, turned(across, SW, 1))
    head, tail = folded(across)
    s_inverse[:rows] = inverted(head, s_free[:rows])
    s_inverse[rows:] = inverted(tail, s_free[rows:])

    lane = lanes_of((8, lanes))
    last_plane = lane >= lanes - SW
    first_plane = lane < SW
    starts = range(0, tall, 8)

    def strip_pairs():
        for c in range(3):
            for r in starts:
                value = s_disp[c, r : r + 8]
                ahead = turned(value, -1, 1)
                s_part[2 * c, r : r + 8] = value + ahead
                s_part[2 * c + 1, r : r + 8] = ahead - value
        for k in range(6):
            for r in starts:
                value = s_part[k, r : r + 8]
                beside = jnp.where(last_plane, 0.0, turned(value, -SW, 1))
                s_pairs[2 * k, r : r + 8] = value + beside
                s_pairs[2 * k + 1, r : r + 8] = beside - value
            for n in (2 * k, 2 * k + 1):
                s_pairs[n, tall : tall + 1] = s_pairs[n, 0:1]

    for c in range(3):
        s_disp[c] = s_inverse[...] * s_basis[0, c]
    strip_pairs()
    for j in range(4):
        for r in starts:
            u = []
            for c in range(3):
                modes = {}
                for g in range(2):
                    for alpha in range(2):
                        k = 2 * (2 * c + g) + alpha
                        now = s_pairs[k, r : r + 8]
                        after = s_pairs[k, r + 1 : r + 9]
                        if (alpha, g) != (0, 0):
                            modes[alpha, 0, g] = now + after
                        modes[alpha, 1, g] = after - now
                u.append(modes)
            f = element_forces(u, s_modulus[r : r + 8])
            for c in range(3):
                for g in range(2):
                    for alpha in range(2):
                        k = 2 * (2 * c + g) + alpha
                        diff = f[c][alpha, 1, g]
                        if (alpha, g) == (0, 0):
                            s_near[k, r : r + 8] = -diff
                            s_far[k, r + 8 : r + 16] = diff
                        else:
                            total = f[c][alpha, 0, g]
                            s_near[k, r : r + 8] = total - diff
                            s_far[k, r + 8 : r + 16] = total + diff
        for k in range(12):
            s_far[k, 7:8] = s_far[k, tall + 7 : tall + 8]
        for k in range(6):
            for r in starts:
                total = s_near[2 * k, r : r + 8] + s_far[2 * k, r + 7 : r + 15]
                diff = s_near[2 * k + 1, r : r + 8] + s_far[2 * k + 1, r + 7 : r + 15]
                upper = jnp.where(first_plane, 0.0, turned(total + diff, SW, 1))
                s_part[k, r : r + 8] = (total - diff) + upper
        for c in range(3):
            for r in starts:
                total = s_part[2 * c, r : r + 8]
                diff = s_part[2 * c + 1, r : r + 8]
                out = (total - diff) + turned(total + diff, 1, 1)
                new = s_free[r : r + 8] * out - SHIFTS[j] * s_basis[j, c, r : r + 8]
                s_basis[j + 1, c, r : r + 8] = new
                if j < 3:
                    s_disp[c, r : r + 8] = s_inverse[r : r + 8] * new
        if j < 3:
            strip_pairs()

    def close_rows(pairs, p):
        for k in range(6):
            pairs[k, p, tall : tall + 1] = pairs[k, p, 0:1]

    for pairs in (pairs_0, pairs_1):
        for k in range(6):
            pairs[k, count] = jnp.zeros(pairs.shape[2:], jnp.float32)

    def start_plane(p, carry):
        disp = {(r, c): inverse[p, r : r + 8] * basis_0[c, p, r : r + 8] for r in starts for c in range(3)}
        ahead = {key: turned(value, -1, 1) for key, value in disp.items()}
        for (r, c), value in disp.items():
            pairs_0[2 * c, p, r : r + 8] = value + ahead[r, c]
            pairs_0[2 * c + 1, p, r : r + 8] = ahead[r, c] - value
        close_rows(pairs_0, p)
        return carry

    lax.fori_loop(0, count, start_plane, 0)

    def along_rows(pairs, p, r):
        result = []
        for k in range(6):
            now = pairs[k, p, r : r + 8]
            after = pairs[k, p, r + 1 : r + 9]
            result.append((now + after, after - now))
        return result

    def elements(pairs, p, r):
        upper_rows = along_rows(pairs, p + 1, r)
        u = []
        for c in range(3):
            modes = {}
            for g in range(2):
                for beta_ in range(2):
                    k = 2 * (2 * c + g) + beta_
                    now = kept[k, r : r + 8]
                    above = upper_rows[2 * c + g][beta_]
                    if (beta_, g) != (0, 0):
                        modes[0, beta_, g] = now + above
                    modes[1, beta_, g] = above - now
                    kept[k, r : r + 8] = above
            u.append(modes)
        f = element_forces(u, modulus[p, r : r + 8])
        for c in range(3):
            for g in range(2):
                t_beta = []
                for beta_ in range(2):
                    k = 2 * (2 * c + g) + beta_
                    diff = f[c][1, beta_, g]
                    before = carried[k, r : r + 8]
                    if (beta_, g) == (0, 0):
                        t_beta.append(before - diff)
                        carried[k, r : r + 8] = diff
                    else:
                        total = f[c][0, beta_, g]
                        t_beta.append(before + (total - diff))
                        carried[k, r : r + 8] = total + diff
                near[2 * c + g, r : r + 8] = t_beta[0] - t_beta[1]
                far[2 * c + g, r + 8 : r + 16] = t_beta[0] + t_beta[1]

    def close_far():
        for k in range(6):
            far[k, 7:8] = far[k, tall + 7 : tall + 8]

    def turn_sums(r):
        both = []
        for c in range(3):
            total = near[2 * c, r : r + 8] + far[2 * c, r + 7 : r + 15]
            diff = near[2 * c + 1, r : r + 8] + far[2 * c + 1, r + 7 : r + 15]
            both.append((total - diff, turned(total + diff, 1, 1)))
        return both

    def new_rows(j, p, r, both):
        open_nodes = free[p, r : r + 8]
        inv = inverse[p, r : r + 8]
        disp = []
        for c, (here, moved) in enumerate(both):
            new = open_nodes * (here + moved) - SHIFTS[j] * basis[j][c, p, r : r + 8]
            basis[j + 1][c, p, r : r + 8] = new
            if j < 3:
                disp.append(inv * new)
        return [(value, turned(value, -1, 1)) for value in disp]

    def put_pairs(pairs, p, r, disp):
        for c, (value, ahead) in enumerate(disp):
            pairs[2 * c, p, r : r + 8] = value + ahead
            pairs[2 * c + 1, p, r : r + 8] = ahead - value

    for j in range(4):
        source, target = (pairs_0, pairs_1) if j % 2 == 0 else (pairs_1, pairs_0)
        low = gx * j
        high = count - 1 - j + gx * (j + 1)
        for r in starts:
            for k, both in enumerate(along_rows(source, low, r)):
                for beta_ in range(2):
                    kept[2 * k + beta_, r : r + 8] = both[beta_]
                    carried[2 * k + beta_, r : r + 8] = jnp.zeros((8, lanes), jnp.float32)

        def only_elements(p, state, source=source):
            for r in starts:
                elements(source, p, r)
            close_far()
            return state

        def layer(p, state, j=j, source=source, target=target):
            waiting = {0: turn_sums(0)}
            pending = None
            for r in starts:
                if r + 8 < tall:
                    waiting[r + 8] = turn_sums(r + 8)
                disp = new_rows(j, p - 1, r, waiting.pop(r))
                elements(source, p, r)
                if pending is not None:
                    put_pairs(target, p - 1, *pending)
                pending = (r, disp)
            put_pairs(target, p - 1, *pending)
            if j < 3:
                close_rows(target, p - 1)
            close_far()
            return state

        lax.fori_loop(low, low + 1 + gx, only_elements, 0)
        lax.fori_loop(low + 1 + gx, high, layer, 0)
        for r in starts if j < 3 else range(0, rows, 8):
            disp = new_rows(j, high - 1, r, turn_sums(r))
            put_pairs(target, high - 1, r, disp)
        if j < 3:
            close_rows(target, high - 1)

    order = [(i, k) for i in range(4) for k in range(i, 5)]
    zero = jnp.zeros((8, lanes), jnp.float32)

    def add_dots(p, sums):
        plane = mine + p
        sums = list(sums)
        for r in range(0, rows, 8):
            inv = inverse[plane, r : r + 8]
            scale[p, r : r + 8] = inv
            for c in range(3):
                ys = [basis[i][c, plane, r : r + 8] for i in range(5)]
                ws = [inv * y for y in ys[:4]]
                for i in range(5):
                    fields[i, c, p, r : r + 8] = ys[i]
                for n, (i, k) in enumerate(order):
                    sums[n] = sums[n] + ws[i] * ys[k]
        return tuple(sums)

    main = lax.fori_loop(0, planes, add_dots, (zero,) * len(order))
    extra = [zero] * len(order)
    for r in range(0, rows, 8):
        inv = s_inverse[r : r + 8]
        strip_scale[r : r + 8] = inv
        for c in range(3):
            ys = [s_basis[i, c, r : r + 8] for i in range(5)]
            ws = [inv * y for y in ys[:4]]
            for i in range(5):
                strip_fields[i, c, r : r + 8] = ys[i]
            for n, (i, k) in enumerate(order):
                extra[n] = extra[n] + ws[i] * ys[k]
    place = lax.rem(lane, SW)
    own_lanes = (place >= 4) & (place < 12) & (lane // (SW * planes) == gx)
    sums = [
        jnp.where(lane < lanes - 8, value, 0.0) + jnp.where(own_lanes, more, 0.0) for value, more in zip(main, extra)
    ]
    spread(sums, dots)


def combine_kernel(dots, basis, strips, scale, strip_scale, displacement, residual, ends):
    order = [(i, k) for i in range(4) for k in range(i, 5)]
    gram = {}
    for value, (i, k) in zip(gathered(dots, len(order)), order):
        gram[i, k] = gram[k, i] = value
    zero = jnp.zeros((1, 1), jnp.float32)
    one = jnp.ones((1, 1), jnp.float32)
    res = [one]
    search = [one]
    disp = []
    res_dot = gram[0, 0]
    for iteration in range(4):
        image = [zero] * (iteration + 2)
        for i, value in enumerate(search):
            image[i] = image[i] + SHIFTS[i] * value
            image[i + 1] = image[i + 1] + value
        curve = zero
        for i, left in enumerate(search):
            inner = zero
            for k, right in enumerate(image):
                inner = inner + gram[i, k] * right
            curve = curve + left * inner
        step = res_dot / curve
        disp = [d + step * s for d, s in zip(disp + [zero], search)]
        res = [r - step * q for r, q in zip(res + [zero], image)]
        if iteration < 3:
            new_dot = zero
            for i, left in enumerate(res):
                inner = zero
                for k, right in enumerate(res):
                    inner = inner + gram[i, k] * right
                new_dot = new_dot + left * inner
            search = [r + new_dot / res_dot * s for r, s in zip(res, search + [zero])]
            res_dot = new_dot
    planes, rows, lanes = scale.shape
    disp = [jnp.broadcast_to(d, (8, lanes)) for d in disp]
    res = [jnp.broadcast_to(r, (8, lanes)) for r in res]

    def combined(ys, inv):
        first = disp[0] * ys[0]
        second = res[0] * ys[0]
        for i in range(1, 5):
            second = second + res[i] * ys[i]
            if i < 4:
                first = first + disp[i] * ys[i]
        return inv * first, second

    gx = lax.axis_index("gx")
    for r in range(0, rows, 8):
        for c in range(3):
            both = combined([strips[i, c, r : r + 8] for i in range(5)], strip_scale[r : r + 8])
            for n, value in enumerate(both):
                ends[3 * n + c, r : r + 8] = either(gx, value, turned(value, lanes // 2, 1))
    lane = lanes_of((8, lanes))
    for p in range(planes):
        for r in range(0, rows, 8):
            inv = scale[p, r : r + 8]
            for c in range(3):
                both = combined([basis[i, c, p, r : r + 8] for i in range(5)], inv)
                for n, out in enumerate((displacement, residual)):
                    end = turned(ends[3 * n + c, r : r + 8], lanes - 8 - (SW * p + 4), 1)
                    out[c, p, r : r + 8] = jnp.where(lane < lanes - 8, both[n], end)


def call(kernel, outs, *args, scratch=()):
    return pl.pallas_call(
        kernel,
        out_shape=tuple(jax.ShapeDtypeStruct(shape, jnp.float32) for shape in outs),
        in_specs=[pl.BlockSpec(memory_space=pltpu.VMEM)] * len(args),
        out_specs=tuple(pl.BlockSpec(memory_space=pltpu.VMEM) for _ in outs),
        scratch_shapes=list(scratch),
        compiler_params=pltpu.CompilerParams(vmem_limit_bytes=VMEM_LIMIT),
    )(*args)


def swapped(value, axis, first):
    count = lax.axis_size(axis)
    pairs = [(i, i + 1) for i in range(first, count - 1, 2)]
    if not pairs:
        return jnp.zeros_like(value)
    return lax.ppermute(value, axis, pairs + [(j, i) for i, j in pairs])


def paired_shards(density, fixed_mask, load_mask, load_values):
    planes, rows, lanes = density.shape
    devices = 1
    for axis in AXES:
        devices *= lax.axis_size(axis)
    grid = (rows * lax.axis_size("gy"), lanes * lax.axis_size("gz"))
    count = 2 * planes
    wide, tall = rows + 2 * FACE, rows + FACE
    face = (4 * planes, FACE, lanes)
    row = (devices, 1, lanes)
    f32 = jnp.float32
    density_other = swapped(density, "gx", 0)
    density_own, nodes = call(
        node_kernel, (density.shape, (4 * planes, rows, lanes)), density, fixed_mask, load_mask, load_values
    )
    nodes_other = swapped(nodes, "gx", 0)
    send_a, send_b = call(face_kernel, (face, face), density_own, density_other, nodes)
    window, tails, strips = call(
        strip_kernel,
        ((count, wide, lanes), (4 * planes, FACE, lanes), (wide + 2 * tall, lanes)),
        density_own, density_other, nodes, swapped(send_a, "gy", 0), swapped(send_b, "gy", 1),
    )
    from_a, from_b = swapped(strips, "gz", 0), swapped(strips, "gz", 1)
    first, strip_v, strip_g, node_strips, dots = call(
        functools.partial(filter_kernel, grid),
        ((count, wide, lanes), (wide, lanes), (wide, lanes), (4 * tall + 4 * planes * FACE, lanes), row),
        window, tails, strips, from_a, from_b,
    )
    strips_other = swapped(node_strips, "gx", 0)
    dots = lax.all_to_all(dots, AXES, 0, 0, tiled=True)
    diagonal = float(element_table()[0, 0, 0, 0])
    plane, taller = (tall, lanes), (tall + 8, lanes)
    many = (count,) + plane
    filtered, basis, strip_basis, scale, strip_scale, dots = call(
        functools.partial(solve_kernel, grid, diagonal),
        ((planes, rows, lanes), (5, 3, planes, rows, lanes), (5, 3, rows, lanes), (planes, rows, lanes), (rows, lanes), row),
        window, first, strip_v, strip_g, dots, nodes, nodes_other, node_strips, strips_other,
        scratch=[
            pltpu.VMEM(shape, f32)
            for shape in (
                *(((3,) + many,) * 5), many, many, many, (6, count + 1) + taller, (6, count + 1) + taller, (12,) + plane, (12,) + plane, (6,) + plane, (6,) + taller,
                (5, 3) + plane, plane, plane, plane, (12,) + taller, (12,) + plane, (12,) + taller, (6,) + plane, (3,) + plane,
            )
        ],
    )
    dots = lax.all_to_all(dots, AXES, 0, 0, tiled=True)
    displacement, residual = call(
        combine_kernel, (load_values.shape, load_values.shape), dots, basis, strip_basis, scale, strip_scale,
        scratch=[pltpu.VMEM((6, rows, lanes), f32)],
    )
    return (filtered, displacement, residual)


def shards(density, fixed_mask, load_mask, load_values):
    planes, rows, lanes = density.shape
    if lax.axis_size("gx") == 2 and 2 * planes * SW == lanes and lanes == 128 and rows % 8 == 0:
        return paired_shards(density, fixed_mask, load_mask, load_values)
    return general_shards(density, fixed_mask, load_mask, load_values)


def solution(mesh):
    return jax.shard_map(
        shards,
        mesh=mesh,
        in_specs=(
            P("gx", "gy", "gz"),
            P("gx", "gy", "gz"),
            P("gx", "gy", "gz"),
            P(None, "gx", "gy", "gz"),
        ),
        out_specs=(P("gx", "gy", "gz"), P(None, "gx", "gy", "gz"), P(None, "gx", "gy", "gz")),
        check_vma=False,
    )
```
